128 devices in a mesh: lon: 8 (over x, z_hi), lat: 16 (over y, z_lo, core).
Axes of the slice: x: 4, y: 4, z: 4 (z_hi: 2, z_lo: 2; z = z_hi * 2 + z_lo), core: 2. Of those that a mesh axis runs over, the one named last changes fastest.
Arguments:
- tokens: bfloat16 [4, 192, 192, 192], P(None, 'lat', 'lon'), may hold values from -6 to 6
- gain_one: float32 [192], replicated, may hold values from 0.5 to 1.5
- w_qkv: bfloat16 [192, 576], replicated, may hold values from -0.4375 to 0.4375
- w_proj: bfloat16 [192, 192], replicated, may hold values from -0.4375 to 0.4375
- bias_table: float32 [16, 2, 6, 144, 144], P('lat'), may hold values from -4 to 4
- gain_two: float32 [192], replicated, may hold values from 0.5 to 1.5
- w_fc1: bfloat16 [192, 768], replicated, may hold values from -0.4375 to 0.4375
- w_fc2: bfloat16 [768, 192], replicated, may hold values from -0.21875 to 0.21875
- gain_merge: float32 [768], replicated, may hold values from 0.5 to 1.5
- w_merge: bfloat16 [768, 384], replicated, may hold values from -0.21875 to 0.21875
- cotangent: bfloat16 [4, 96, 96, 384], P(None, 'lat', 'lon'), may hold values from -6 to 6
Outputs:
- merged: bfloat16 [4, 96, 96, 384], P(None, 'lat', 'lon')
- grad_tokens: bfloat16 [4, 192, 192, 192], P(None, 'lat', 'lon')
- grad_qkv: float32 [192, 576], replicated
- grad_proj: float32 [192, 192], replicated
- grad_fc1: float32 [192, 768], replicated
- grad_fc2: float32 [768, 192], replicated
- grad_merge: float32 [768, 384], replicated
- grad_bias: float32 [16, 2, 6, 144, 144], P('lat')
The draws below stay inside these ranges and needn't reach their ends.
All inputs are finite; a program needn't handle non-finite values.
Results may differ from the reference program's by a relative error of at most 0.02.
Values may be sent and summed in bfloat16 or wider, within the bound.
No kernel may reach another device: no remote copies, remote signals or barrier semaphores. Data moves between devices by JAX's collectives and lax.ppermute only.
A program may use at most 128 MiB of HBM per device.

```python
import jax
import jax.numpy as jnp
from jax import lax

D = 192
HEADS = 6
FF = 768
MERGED = 384
LEVELS = 4
WLAT = 12
WLON = 6
WT = 144
LAT = 192
LON = 192
LATWIN = 16
ZWIN = 2


def block_scale(rng, extent, pieces, low, top_value):
    level, own = 1.0, jax.random.fold_in(rng, 6)
    for axis_at, blocks in pieces:
        steps = jnp.exp(jax.random.uniform(jax.random.fold_in(own, axis_at), (blocks,), jnp.float32, low / len(pieces), top_value / len(pieces)))
        level = level * jnp.repeat(steps, extent[axis_at] // blocks).reshape([-1 if axis == axis_at else 1 for axis in range(len(extent))])
    return level


def bell_draw(stream_key, dims, scale, bound, split=(), held_as=jnp.bfloat16):
    entries = scale * jax.random.normal(stream_key, dims, jnp.float32)
    if split:
        entries = entries * block_scale(stream_key, dims, split, -0.22, 0.18)
    return jnp.clip(entries, -bound, bound).astype(held_as)


def setup_inputs(seed: int = 0) -> dict:
    key_of = jax.random.split(jax.random.key(seed), 12)
    tokens = bell_draw(key_of[0], (LEVELS, LAT, LON, D), 1.0, 6.0, ((1, 16), (2, 8)))
    gain_one = jnp.clip(1.0 + 0.1 * jax.random.normal(key_of[1], (D,), jnp.float32), 0.5, 1.5)
    w_qkv = bell_draw(key_of[2], (D, 3 * D), D ** -0.5, 0.4375)
    w_proj = bell_draw(key_of[3], (D, D), D ** -0.5, 0.4375)
    bias_table = bell_draw(key_of[4], (LATWIN, ZWIN, HEADS, WT, WT), 1.0, 4.0, ((0, 16),), jnp.float32)
    gain_two = jnp.clip(1.0 + 0.1 * jax.random.normal(key_of[5], (D,), jnp.float32), 0.5, 1.5)
    w_fc1 = bell_draw(key_of[6], (D, FF), D ** -0.5, 0.4375)
    w_fc2 = bell_draw(key_of[7], (FF, D), FF ** -0.5, 0.21875)
    gain_merge = jnp.clip(1.0 + 0.1 * jax.random.normal(key_of[8], (4 * D,), jnp.float32), 0.5, 1.5)
    w_merge = bell_draw(key_of[9], (4 * D, MERGED), (4 * D) ** -0.5, 0.21875)
    cotangent = bell_draw(key_of[10], (LEVELS, LAT // 2, LON // 2, MERGED), 1.0, 6.0, ((1, 16), (2, 8)))
    return {"tokens": tokens, "gain_one": gain_one, "w_qkv": w_qkv, "w_proj": w_proj, "bias_table": bias_table, "gain_two": gain_two, "w_fc1": w_fc1, "w_fc2": w_fc2, "gain_merge": gain_merge, "w_merge": w_merge, "cotangent": cotangent}


EPS = 1e-05

def rounded(values):
    return lax.optimization_barrier(values.astype(jnp.bfloat16))

def layer_norm(values, gain):
    center = values - lax.optimization_barrier(jnp.mean(values, axis=-1, keepdims=True))
    spread = lax.optimization_barrier(jnp.mean(center * center, axis=-1, keepdims=True))
    return center * lax.rsqrt(spread + EPS) * gain

def norm_back(values, gain, upstream):
    return jax.vjp(lambda inner: layer_norm(inner, gain), values)[1](upstream)[0]

def gelu_back(pre_act, upstream):
    return jax.vjp(jax.nn.gelu, pre_act)[1](upstream)[0]

def partition(field):
    levels, rows, cols, features = field.shape
    blocks = field.reshape(levels // 2, 2, rows // WLAT, WLAT, cols // WLON, WLON, features)
    return blocks.transpose(2, 0, 4, 1, 3, 5, 6).reshape(rows // WLAT, levels // 2, cols // WLON, 2 * WLAT * WLON, features)

def unpartition(windows):
    lat_wins, level_wins, lon_wins, win_tokens, features = windows.shape
    blocks = windows.reshape(lat_wins, level_wins, lon_wins, 2, WLAT, WLON, features)
    return blocks.transpose(1, 3, 0, 4, 2, 5, 6).reshape(level_wins * 2, lat_wins * WLAT, lon_wins * WLON, features)

def to_quads(field):
    levels, rows, cols, features = field.shape
    blocks = field.reshape(levels, rows // 2, 2, cols // 2, 2, features)
    return blocks.transpose(0, 1, 3, 2, 4, 5).reshape(levels, rows // 2, cols // 2, 4 * features)

def from_quads(field):
    levels, rows, cols, features = field.shape
    blocks = field.reshape(levels, rows, cols, 2, 2, features // 4)
    return blocks.transpose(0, 1, 3, 2, 4, 5).reshape(levels, rows * 2, cols * 2, features // 4)

def region_mask(wrapped, level_wins):
    positions = jnp.arange(2 * WLAT * WLON)
    upper = positions // (WLAT * WLON)
    row_in = positions // WLON % WLAT
    last_level = (jnp.arange(level_wins) == level_wins - 1)[:, None]
    level_label = (last_level & (upper == 1)[None, :]).astype(jnp.int32)
    row_label = (wrapped & (row_in >= WLAT // 2)).astype(jnp.int32)
    labels = 2 * level_label + row_label[None, :]
    return (labels[:, :, None] == labels[:, None, :]).astype(jnp.float32)

def contract(left, right):
    return jnp.dot(left.reshape(-1, left.shape[-1]).T, right.reshape(-1, right.shape[-1]), preferred_element_type=jnp.float32)

def attend(windows, w_qkv, w_proj, bias_block, region):
    level_wins, lon_wins, win_tokens, features = windows.shape
    head_dim = features // HEADS
    qkv_proj = rounded(jnp.dot(windows, w_qkv, preferred_element_type=jnp.float32))
    qkv_proj = qkv_proj.reshape(level_wins, lon_wins, win_tokens, 3, HEADS, head_dim)
    query_part = qkv_proj[:, :, :, 0].astype(jnp.float32)
    key_part = qkv_proj[:, :, :, 1].astype(jnp.float32)
    value_part = qkv_proj[:, :, :, 2].astype(jnp.float32)
    scores = jnp.einsum('zlqhc,zlkhc->zlhqk', query_part, key_part) * head_dim ** (-0.5) + bias_block[:, None]
    raised = jnp.exp(scores) * region[:, None, None]
    softmax = raised / lax.optimization_barrier(jnp.sum(raised, axis=-1, keepdims=True))
    soft_round = rounded(softmax).astype(jnp.float32)
    mixed_heads = jnp.einsum('zlhqk,zlkhc->zlqhc', soft_round, value_part).astype(jnp.bfloat16)
    mixed_heads = mixed_heads.reshape(level_wins, lon_wins, win_tokens, features)
    attended = jnp.dot(mixed_heads, w_proj, preferred_element_type=jnp.float32).astype(jnp.bfloat16)
    return (attended, (qkv_proj, softmax, mixed_heads))

def attend_back(windows, w_qkv, w_proj, stored, upstream):
    qkv_proj, softmax, mixed_heads = stored
    level_wins, lon_wins, win_tokens, features = windows.shape
    head_dim = features // HEADS
    grad_proj = contract(mixed_heads, upstream)
    d_mixed = rounded(jnp.dot(upstream, w_proj.T, preferred_element_type=jnp.float32)).astype(jnp.float32)
    d_mixed = d_mixed.reshape(level_wins, lon_wins, win_tokens, HEADS, head_dim)
    query_part = qkv_proj[:, :, :, 0].astype(jnp.float32)
    key_part = qkv_proj[:, :, :, 1].astype(jnp.float32)
    value_part = qkv_proj[:, :, :, 2].astype(jnp.float32)
    soft_round = rounded(softmax).astype(jnp.float32)
    d_soft = jnp.einsum('zlqhc,zlkhc->zlhqk', d_mixed, value_part)
    d_value = jnp.einsum('zlhqk,zlqhc->zlkhc', soft_round, d_mixed)
    d_scores = softmax * (d_soft - lax.optimization_barrier(jnp.sum(d_soft * softmax, axis=-1, keepdims=True)))
    grad_bias = lax.optimization_barrier(jnp.sum(d_scores, axis=1))
    d_scaled = rounded(d_scores * head_dim ** (-0.5)).astype(jnp.float32)
    d_query = jnp.einsum('zlhqk,zlkhc->zlqhc', d_scaled, key_part)
    d_key = jnp.einsum('zlhqk,zlqhc->zlkhc', d_scaled, query_part)
    d_qkv = jnp.stack([d_query, d_key, d_value], axis=3).astype(jnp.bfloat16)
    d_qkv = d_qkv.reshape(level_wins, lon_wins, win_tokens, 3 * features)
    grad_qkv = contract(windows, d_qkv)
    d_windows = jnp.dot(d_qkv, w_qkv.T, preferred_element_type=jnp.float32).astype(jnp.bfloat16)
    return (d_windows, grad_qkv, grad_proj, grad_bias)

def reference(tokens, gain_one, w_qkv, w_proj, bias_table, gain_two, w_fc1, w_fc2, gain_merge, w_merge, cotangent):
    levels, lat_all, lon_all, features = tokens.shape
    half_lat = WLAT // 2
    half_lon = WLON // 2
    normed_in = layer_norm(tokens.astype(jnp.float32), gain_one).astype(jnp.bfloat16)
    windows = partition(jnp.roll(normed_in, (-1, -half_lat, -half_lon), (0, 1, 2)))
    lat_wins = windows.shape[0]
    level_wins = windows.shape[1]

    def forward_row(packed):
        window_row, bias_block, row_index = packed
        region = region_mask(row_index == lat_wins - 1, level_wins)
        return attend(window_row, w_qkv, w_proj, bias_block, region)[0]
    attended = lax.map(forward_row, (windows, bias_table, jnp.arange(lat_wins)))
    attention = jnp.roll(unpartition(attended), (1, half_lat, half_lon), (0, 1, 2))
    residual = (tokens.astype(jnp.float32) + attention.astype(jnp.float32)).astype(jnp.bfloat16)
    mlp_in = layer_norm(residual.astype(jnp.float32), gain_two).astype(jnp.bfloat16)
    pre_act = jnp.dot(mlp_in, w_fc1, preferred_element_type=jnp.float32)
    activated = jax.nn.gelu(pre_act).astype(jnp.bfloat16)
    block_out = (residual.astype(jnp.float32) + jnp.dot(activated, w_fc2, preferred_element_type=jnp.float32)).astype(jnp.bfloat16)
    quad_feats = to_quads(block_out).astype(jnp.float32)
    merged_normed = layer_norm(quad_feats, gain_merge).astype(jnp.bfloat16)
    merged = jnp.dot(merged_normed, w_merge, preferred_element_type=jnp.float32).astype(jnp.bfloat16)
    merge_sum = contract(merged_normed, cotangent)
    d_normed_merge = jnp.dot(cotangent, w_merge.T, preferred_element_type=jnp.float32)
    d_block = from_quads(norm_back(quad_feats, gain_merge, d_normed_merge)).astype(jnp.bfloat16)
    fc2_sum = contract(activated, d_block)
    d_act = jnp.dot(d_block, w_fc2.T, preferred_element_type=jnp.float32)
    d_pre = gelu_back(pre_act, d_act).astype(jnp.bfloat16)
    fc1_sum = contract(mlp_in, d_pre)
    d_mlp_in = jnp.dot(d_pre, w_fc1.T, preferred_element_type=jnp.float32)
    d_residual = (d_block.astype(jnp.float32) + norm_back(residual.astype(jnp.float32), gain_two, d_mlp_in)).astype(jnp.bfloat16)
    d_attended = partition(jnp.roll(d_residual, (-1, -half_lat, -half_lon), (0, 1, 2)))

    def backward_row(carry, packed):
        window_row, bias_block, row_index, upstream = packed
        region = region_mask(row_index == lat_wins - 1, level_wins)
        stored = attend(window_row, w_qkv, w_proj, bias_block, region)[1]
        d_row, qkv_part, proj_part, bias_part = attend_back(window_row, w_qkv, w_proj, stored, upstream)
        return ((carry[0] + qkv_part, carry[1] + proj_part), (d_row, bias_part))
    start = (jnp.zeros((features, 3 * features), jnp.float32), jnp.zeros((features, features), jnp.float32))
    sums, rows_out = lax.scan(backward_row, start, (windows, bias_table, jnp.arange(lat_wins), d_attended))
    qkv_sum, proj_sum = sums
    d_rows, bias_sum = rows_out
    d_normed = jnp.roll(unpartition(d_rows), (1, half_lat, half_lon), (0, 1, 2))
    grad_tokens = (d_residual.astype(jnp.float32) + norm_back(tokens.astype(jnp.float32), gain_one, d_normed.astype(jnp.float32))).astype(jnp.bfloat16)
    grad_scale = (levels * lat_all * lon_all) ** (-0.5)
    bias_scale = 2 * WLAT * WLON * (lon_all // WLON) ** (-0.5)
    return (merged, grad_tokens, qkv_sum * grad_scale, proj_sum * grad_scale, fc1_sum * grad_scale, fc2_sum * grad_scale, merge_sum * grad_scale, bias_sum * bias_scale)
```

```python
import functools

import jax
import jax.numpy as jnp
import numpy as np
from jax import lax
from jax.experimental import pallas as pl
from jax.experimental.pallas import tpu as pltpu
from jax.sharding import PartitionSpec as P

F32 = jnp.float32
BF16 = jnp.bfloat16
EPS = 1e-05
D = 192
HEADS = 6
HD = 32
WT = 144
HQ = HEADS * WT
FF = 768
MG = 384
SCALE = HD ** (-0.5)
OFF = -1e30
GROUP = 2
CHUNK = 48
ROWS = 64
N_CHUNK = 128


def one_hot(shape, pairs):
    table = np.zeros(shape, np.float32)
    for row, col in pairs:
        table[row, col] = 1.0
    return jnp.asarray(table, BF16)


def pack_map():
    pairs = [(r * 9 + c, r * 24 + c) for r in range(6) for c in range(9)]
    pairs += [(64 + r * 3 + c, r * 24 + 21 + c) for r in range(6) for c in range(3)]
    return one_hot((96, 144), pairs)


def pack_cot_map():
    pairs = []
    for lev in range(4):
        for r in range(3):
            for c in range(12):
                pairs.append((lev * 128 + r * 16 + c, ((3 + r) * 12 + c) * 4 + lev))
                pairs.append((lev * 128 + 48 + r * 16 + c, (r * 12 + c) * 4 + lev))
            for c in range(2):
                pairs.append((lev * 128 + 96 + r * 2 + c, ((3 + r) * 12 + c) * 4 + lev))
                pairs.append((lev * 128 + 112 + r * 2 + c, (r * 12 + c) * 4 + lev))
    return one_hot((512, 288), pairs)


def window_map():
    pairs = []
    for win in range(6):
        for row in range(12):
            for c in range(6):
                e, r = 6 * win + c, row % 6
                upper = row < 6
                if e < 3:
                    src = (352 if upper else 448) + r * 3 + e
                elif e < 27:
                    src = (0 if upper else 144) + r * 24 + e - 3
                else:
                    src = (288 if upper else 384) + r * 9 + e - 27
                pairs.append((win * 72 + row * 6 + c, src))
    return one_hot((432, 480), pairs)


def cot_map():
    pairs = []
    for r in range(6):
        for p in range(13):
            if p < 11:
                src = r * 16 + p + 1
            else:
                src = (96 if r < 3 else 112) + r % 3 * 2 + p - 11
            pairs.append((r * 13 + p, src))
    return one_hot((80, 128), pairs)


def quad_pairs():
    pairs = []
    for ro in range(2):
        for co in range(2):
            for pr in range(6):
                for p in range(13):
                    row, e = 2 * pr + ro, 5 + 2 * p + co
                    if e == 5:
                        src = 288 + row
                    elif e == 30:
                        src = 304 + row
                    else:
                        src = (e - 6) // 6 * 72 + row * 6 + (e - 6) % 6
                    pairs.append(((2 * ro + co) * 80 + pr * 13 + p, src))
    return pairs


def quad_map():
    return one_hot((320, 320), quad_pairs())


def back_map():
    return one_hot((288, 320), [(s, d) for d, s in quad_pairs() if s < 288])


def out_map():
    pairs = []
    for row in range(12):
        for e in range(24):
            src = e // 6 * 72 + row * 6 + e % 6
            r = row % 6
            if e < 21:
                dst = (0 if row < 6 else 144) + r * 24 + e + 3
            else:
                dst = (288 if row < 6 else 320) + r * 3 + e - 21
            pairs.append((dst, src))
    return one_hot((352, 288), pairs)


def merged_map():
    pairs = []
    for r in range(6):
        for p in range(11):
            pairs.append(((0 if r < 3 else 48) + r % 3 * 16 + p + 1, r * 13 + p))
        pairs.append(((96 if r < 3 else 112) + r % 3, r * 13 + 11))
    return one_hot((128, 80), pairs)


def place_map():
    return one_hot((144, 32), [(r * 24 + c, r * 3 + c) for r in range(6) for c in range(3)])


def place_merged_map():
    pairs = []
    for lev in range(4):
        for r in range(6):
            for c in range(12):
                if c:
                    src = (192 if r < 3 else 0) + lev * 48 + r % 3 * 16 + c
                else:
                    src = (448 if r < 3 else 384) + lev * 16 + r % 3
                pairs.append(((r * 12 + c) * 4 + lev, src))
    return one_hot((288, 512), pairs)


def head_mask():
    return one_hot((HQ, D), [(h * WT + q, h * HD + c) for h in range(HEADS) for q in range(WT) for c in range(HD)])


def fold_map():
    return one_hot((WT, HQ), [(q, h * WT + q) for h in range(HEADS) for q in range(WT)])


def side_mask():
    return one_hot((WT, D), [(h * 24 + q, h * HD + c) for h in range(HEADS) for q in range(24) for c in range(HD)])


def side_fold():
    pairs = [(li * 16 + r, h * 24 + li * 12 + r) for h in range(HEADS) for li in range(2) for r in range(12)]
    return one_hot((32, WT), pairs)


def side_pick(col, padded):
    step, heads = (16, 1) if padded else (12, HEADS)
    pairs = [
        (h * 2 * step + li * step + r, li * 72 + r * 6 + col)
        for h in range(heads)
        for li in range(2)
        for r in range(12)
    ]
    return one_hot((2 * step * heads, WT), pairs)


def nn(a, b):
    return lax.dot_general(a, b, (((1,), (0,)), ((), ())), preferred_element_type=F32)


def nt(a, b):
    return lax.dot_general(a, b, (((1,), (1,)), ((), ())), preferred_element_type=F32)


def tn(a, b):
    return lax.dot_general(a, b, (((0,), (0,)), ((), ())), preferred_element_type=F32)


def norm_parts(values):
    center = values - jnp.mean(values, axis=-1, keepdims=True)
    rstd = lax.rsqrt(jnp.mean(center * center, axis=-1, keepdims=True) + EPS)
    return center * rstd, rstd


def norm_back(hat, rstd, gain, upstream):
    g = upstream * gain
    return rstd * (g - jnp.mean(g, axis=-1, keepdims=True) - hat * jnp.mean(g * hat, axis=-1, keepdims=True))


LEVEL_AT = ((1, 1), (0, 0), (0, 1), (1, 0))


def pack_kernel(tok, cot, pmap, cmap, dn, rt, lf, dr, dl, here, rows):
    for i in range(72):
        rows[4 * i : 4 * i + 4] = cot[i].astype(F32)
    c_all = nn(cmap[...], rows[...].astype(BF16)).astype(BF16)
    for lev in range(4):
        top = tok[lev, 0:144]
        dn[lev, 0:144] = top
        upper = nn(pmap[...], top).astype(BF16)
        lower = nn(pmap[...], tok[lev, 144:288]).astype(BF16)
        rt[lev, 0:64] = lower[0:64]
        lf[lev] = lower[64:96]
        dr[lev, 0:64] = upper[0:64]
        dl[lev] = upper[64:96]
        c = c_all[lev * 128 : lev * 128 + 128]
        here[lev] = c[0:48]
        for half in range(2):
            part = c[:, half * D : half * D + D]
            dn[lev, 144 + 48 * half : 192 + 48 * half] = part[48:96]
            rt[lev, 64 + 16 * half : 80 + 16 * half] = part[96:112]
            dr[lev, 64 + 16 * half : 80 + 16 * half] = part[112:128]


def label(pos, z, bottom):
    row = ((pos % 72 >= 36) & bottom).astype(jnp.int32)
    return row + (2 * (pos // 72).astype(jnp.int32) if z == 1 else 0)


def split_weights(wqkv, w3, wt3):
    eye = (lax.broadcasted_iota(jnp.int32, (D, D), 0) == lax.broadcasted_iota(jnp.int32, (D, D), 1)).astype(BF16)
    for part in range(3):
        w = wqkv[:, part * D : (part + 1) * D]
        w3[part] = w
        wt3[part] = nt(eye, w).astype(BF16)


def first_kernel(
    bottom_ref, own, dn, rt, lf, dr, dl, cot, bias, gain_one, wqkv, wproj, gain_two, wfc1, wfc2t, gain_merge, wmerge,
    m_win, m_cot, m_quad, m_back, m_head, m_headt, m_fold, m_side, m_sidet, m_sfold, m_pick, m_there,
    grads, merged, tok8, xn, prob, mixed, dout,
    w3, wt3, bias_t, low_cols, high_cols, tok, side, resq, mlpin, act, dgel, blk, dresq, resw, cotq,
):
    split_weights(wqkv, w3, wt3)
    bottom = bottom_ref[0, 0] > 0
    lane = lax.broadcasted_iota(jnp.int32, (1, HQ), 1) % WT
    row = lax.broadcasted_iota(jnp.int32, (WT, 1), 0)
    for z in range(2):
        bias_t[z] = jnp.where(label(row, z, bottom) != label(lane, z, bottom), OFF, bias[z].T)
        low_cols[z] = bias[z, :, 0:128]
        high_cols[z, :, 0 : WT - 128] = bias[z, :, 128:WT]

    for lev in range(4):
        z, li = LEVEL_AT[lev]
        src = jnp.concatenate(
            [own[lev, 144:288], dn[lev, 0:144], rt[lev, 0:64], lf[lev], dr[lev, 0:64], dl[lev]], axis=0
        )
        got = nn(m_win[...], src)
        for win in range(6):
            tok[z * 6 + win, li * 72 : li * 72 + 72] = got[win * 72 : win * 72 + 72]

    g1 = gain_one[...]

    def forward(i, carry):
        ws = [i * GROUP + n for n in range(GROUP)]
        zs = [w // 4 for w in ws]
        ts = [tok[z * 6 + w % 4 + 1] for w, z in zip(ws, zs)]
        xs = [(norm_parts(t)[0] * g1).astype(BF16) for t in ts]
        for w, t, x in zip(ws, ts, xs):
            tok8[w] = t.astype(BF16)
            xn[w] = x
        qs = [nn(x, w3[0]).astype(BF16) for x in xs]
        ks = [nn(x, w3[1]).astype(BF16) for x in xs]
        vts = [nt(wt3[2], x).astype(BF16) for x in xs]
        ss = [nt(k, jnp.concatenate([q] * HEADS, axis=0) * m_head[...]) for q, k in zip(qs, ks)]
        ps = []
        for w, z, score in zip(ws, zs, ss):
            e = jnp.exp(score * SCALE + bias_t[z])
            p = (e * (1.0 / jnp.sum(e, axis=0, keepdims=True))).astype(BF16)
            prob[w] = p
            ps.append(p)
        fulls = [nn(vt, p).astype(BF16) * m_headt[...] for vt, p in zip(vts, ps)]
        mxs = [nt(m_fold[...], full).astype(BF16) for full in fulls]
        for w, t, mx in zip(ws, ts, mxs):
            mixed[w] = mx
            att = nn(mx, wproj[...]).astype(BF16)
            resw[w] = (t + att.astype(F32)).astype(BF16).astype(F32)
        return carry

    lax.fori_loop(0, 8 // GROUP, forward, 0)

    lane = lax.broadcasted_iota(jnp.int32, (1, WT), 1) % 24
    lane = lane // 12 * 72 + lane % 12 * 6
    beside = [(n, z) for n in range(2) for z in range(2)]
    ts = [tok[z * 6 + 5 * n] for n, z in beside]
    xs = [(norm_parts(t)[0] * g1).astype(BF16) for t in ts]
    qs = [nn(x, w3[0]).astype(BF16) for x in xs]
    ks = [nn(x, w3[1]).astype(BF16) for x in xs]
    vts = [nt(wt3[2], x).astype(BF16) for x in xs]
    ss = [nt(k, nn(m_pick[n], q).astype(BF16) * m_side[...]) for q, k, (n, z) in zip(qs, ks, beside)]
    ps = []
    for score, (n, z) in zip(ss, beside):
        every = pl.ds(5 - 5 * n, WT, stride=6)
        table = jnp.concatenate([low_cols[z, every, :], high_cols[z, every, :][:, 0 : WT - 128]], axis=1).T
        table = jnp.where(label(row, z, bottom) != label(lane, z, bottom), OFF, table)
        e = jnp.exp(score * SCALE + table)
        ps.append((e * (1.0 / jnp.sum(e, axis=0, keepdims=True))).astype(BF16))
    fulls = [nn(vt, p).astype(BF16) * m_sidet[...] for vt, p in zip(vts, ps)]
    mxs = [nt(m_sfold[...], full).astype(BF16) for full in fulls]
    for t, mx, (n, z) in zip(ts, mxs, beside):
        att = nn(mx, wproj[...]).astype(BF16)
        there = nn(m_there[n], t.astype(BF16))
        side[n, z] = (there + att.astype(F32)).astype(BF16)

    for lev in range(4):
        z, li = LEVEL_AT[lev]
        src = jnp.concatenate([resw[z * 4 + win, li * 72 : li * 72 + 72] for win in range(4)], axis=0).astype(BF16)
        src = jnp.concatenate([src, side[0, z, li * 16 : li * 16 + 16], side[1, z, li * 16 : li * 16 + 16]], axis=0)
        got = nn(m_quad[...], src).astype(BF16)
        for k in range(4):
            resq[k, lev * 80 : lev * 80 + 80] = got[k * 80 : k * 80 + 80]

    for lev in range(4):
        src = jnp.concatenate(
            [
                cot[lev],
                jnp.concatenate([dn[lev, 144:192], dn[lev, 192:240]], axis=1),
                jnp.concatenate([rt[lev, 64:80], rt[lev, 80:96]], axis=1),
                jnp.concatenate([dr[lev, 64:80], dr[lev, 80:96]], axis=1),
            ],
            axis=0,
        )
        cotq[lev * 80 : lev * 80 + 80] = nn(m_cot[...], src).astype(BF16)

    g2 = gain_two[...]
    inner = np.float32(np.sqrt(2 / np.pi))

    def feed(k, carry):
        res = resq[k].astype(F32)
        hat, _ = norm_parts(res)
        mi = (hat * g2).astype(BF16)
        mlpin[k] = mi
        pre = nn(mi, wfc1[...])
        sq = pre * pre
        t = jnp.tanh(pre * (inner + (inner * 0.044715) * sq))
        half = 0.5 + 0.5 * t
        full = pre * half
        a = full.astype(BF16)
        act[k] = a
        dgel[k] = half + full * (1.0 - half) * (2 * inner + (6 * inner * 0.044715) * sq)
        blk[k] = (res + nt(a, wfc2t[...])).astype(BF16)
        return carry

    lax.fori_loop(0, 4, feed, 0)

    total = 0.0
    for k in range(4):
        total = total + jnp.sum(blk[k].astype(F32), axis=-1, keepdims=True)
    mean = total * (1.0 / 768)
    total = 0.0
    for k in range(4):
        center = blk[k].astype(F32) - mean
        total = total + jnp.sum(center * center, axis=-1, keepdims=True)
    rstd = lax.rsqrt(total * (1.0 / 768) + EPS)
    cq = cotq[...]
    pair = lax.broadcasted_iota(jnp.int32, (320, MG), 0) % 80 % 13
    cq_own = jnp.where(pair < 12, cq.astype(F32), 0.0).astype(BF16)
    out = 0.0
    sum_a = 0.0
    sum_b = 0.0
    for k in range(4):
        gm = gain_merge[:, k * D : k * D + D]
        hat = (blk[k].astype(F32) - mean) * rstd
        mn = (hat * gm).astype(BF16)
        wm = wmerge[k * D : k * D + D]
        out = out + nn(mn, wm)
        gmerge = tn(mn, cq_own).astype(BF16)
        for c in range(4):
            for t in range(3):
                grads[48 + (4 * k + c) * 3 + t, 0:CHUNK] = gmerge[c * CHUNK : (c + 1) * CHUNK, t * 128 : t * 128 + 128]
        g = nt(cq, wm) * gm
        sum_a = sum_a + jnp.sum(g, axis=-1, keepdims=True)
        sum_b = sum_b + jnp.sum(g * hat, axis=-1, keepdims=True)
    merged[...] = out.astype(BF16)
    sum_a = sum_a * (1.0 / 768)
    sum_b = sum_b * (1.0 / 768)
    pair = lax.broadcasted_iota(jnp.int32, (320, D), 0) % 80 % 13
    fc1 = 0.0
    fc2 = 0.0
    for k in range(4):
        wm = wmerge[k * D : k * D + D]
        hat = (blk[k].astype(F32) - mean) * rstd
        g = nt(cq, wm) * gain_merge[:, k * D : k * D + D]
        d = rstd * (g - sum_a - hat * sum_b)
        d = jnp.where(pair == (0 if k % 2 == 0 else 12), 0.0, d)
        db = d.astype(BF16)
        dpre = (nn(db, wfc2t[...]) * dgel[k]).astype(BF16)
        fc2 = fc2 + tn(db, act[k])
        fc1 = fc1 + tn(mlpin[k], dpre)
        dmlp = nt(dpre, wfc1[...])
        hat2, rstd2 = norm_parts(resq[k].astype(F32))
        dresq[k] = (db.astype(F32) + norm_back(hat2, rstd2, g2, dmlp)).astype(BF16)
    for base, value in ((0, fc1.astype(BF16)), (24, fc2.astype(BF16))):
        for t in range(6):
            for c in range(4):
                grads[base + 4 * t + c, 0:CHUNK] = value[c * CHUNK : (c + 1) * CHUNK, t * 128 : t * 128 + 128]

    for lev in range(4):
        z, li = LEVEL_AT[lev]
        src = jnp.concatenate([dresq[k, lev * 80 : lev * 80 + 80] for k in range(4)], axis=0)
        got = nn(m_back[...], src)
        for win in range(4):
            resw[z * 4 + win, li * 72 : li * 72 + 72] = got[win * 72 : win * 72 + 72]
    dout[...] = resw[...].astype(BF16)


def second_kernel(
    grads_in, xn, prob, mixed, datt, wqkv, wproj, m_head, m_headt, m_fold,
    grads, dqkv,
    w3, wt3, gb, weights, biases, sems,
):
    split_weights(wqkv, w3, wt3)
    gb[...] = jnp.zeros_like(gb)

    def backward(i, carry):
        ws = [i * GROUP + n for n in range(GROUP)]
        xs = [xn[w] for w in ws]
        ups = [datt[w] for w in ws]
        qs = [nn(x, w3[0]).astype(BF16) for x in xs]
        vs = [nn(x, w3[2]).astype(BF16) for x in xs]
        kts = [nt(wt3[1], x).astype(BF16) for x in xs]
        dms = [nt(up, wproj[...]).astype(BF16) for up in ups]
        dmbds = [jnp.concatenate([dm] * HEADS, axis=0) * m_head[...] for dm in dms]
        dps = [nt(v, dmbd) for v, dmbd in zip(vs, dmbds)]
        dsbs = []
        for w, dp in zip(ws, dps):
            p = prob[w].astype(F32)
            ds = p * (dp - jnp.sum(dp * p, axis=0, keepdims=True))
            gb[w // 4] += ds
            dsbs.append((ds * SCALE).astype(BF16))
        for w, dmbd in zip(ws, dmbds):
            dqkv[2, w] = nn(prob[w], dmbd).astype(BF16)
        qbds = [jnp.concatenate([q] * HEADS, axis=0) * m_head[...] for q in qs]
        for w, dsb, qbd in zip(ws, dsbs, qbds):
            dqkv[1, w] = nn(dsb, qbd).astype(BF16)
        fulls = [nn(kt, dsb).astype(BF16) * m_headt[...] for kt, dsb in zip(kts, dsbs)]
        for w, full in zip(ws, fulls):
            dqkv[0, w] = nt(m_fold[...], full).astype(BF16)
        return carry

    lax.fori_loop(0, 8 // GROUP, backward, 0)

    xs = xn[...].reshape(8 * WT, D)
    parts = [tn(xs, dqkv[part].reshape(8 * WT, D)) for part in range(3)]
    parts.append(tn(mixed[...].reshape(8 * WT, D), datt[...].reshape(8 * WT, D)))
    value = jnp.concatenate(parts, axis=1).astype(BF16)
    for t in range(6):
        for c in range(4):
            weights[4 * t + c] = value[c * CHUNK : (c + 1) * CHUNK, t * 128 : t * 128 + 128]
    weights[24:32] = jnp.zeros((8, CHUNK, 128), BF16)
    for z in range(2):
        total = gb[z].astype(BF16)
        for t in range(7):
            tile = total[:, t * 128 : min(t * 128 + 128, HQ)]
            if t == 6:
                tile = jnp.concatenate([tile, jnp.zeros((WT, 896 - HQ), BF16)], axis=1)
            for c in range(9):
                biases[(z * 7 + t) * 9 + c] = tile[c * 16 : c * 16 + 16]
    biases[126:128] = jnp.zeros((2, 16, 128), BF16)
    first = pltpu.make_async_copy(weights, grads.at[96:128, 0:CHUNK], sems.at[0])
    other = pltpu.make_async_copy(biases, grads.at[:, CHUNK:ROWS], sems.at[1])
    first.start()
    other.start()
    first.wait()
    other.wait()


def third_kernel(
    tok8, datt, dqkv, merged, gain_one, wqkv, m_out, m_merged,
    keep_t, keep_m, to_rt, to_dn, to_dr,
    gt,
):
    g1 = gain_one[...]
    ws = [wqkv[:, part * D : (part + 1) * D] for part in range(3)]
    for w in range(8):
        dnorm = (nt(dqkv[0, w], ws[0]) + nt(dqkv[1, w], ws[1]) + nt(dqkv[2, w], ws[2])).astype(BF16).astype(F32)
        hat, rstd = norm_parts(tok8[w].astype(F32))
        gt[w] = (datt[w].astype(F32) + norm_back(hat, rstd, g1, dnorm)).astype(BF16).astype(F32)

    for lev in range(4):
        z, li = LEVEL_AT[lev]
        src = jnp.concatenate([gt[z * 4 + win, li * 72 : li * 72 + 72] for win in range(4)], axis=0).astype(BF16)
        got = nn(m_out[...], src).astype(BF16)
        keep_t[lev] = got[0:144]
        to_dn[lev, 0:144] = got[144:288]
        to_rt[lev, 0:32] = got[288:320]
        to_dr[lev, 0:32] = got[320:352]
        got = nn(m_merged[...], merged[lev * 80 : lev * 80 + 80]).astype(BF16)
        keep_m[lev] = got[0:48]
        for half in range(2):
            part = got[:, half * D : half * D + D]
            to_dn[lev, 144 + 48 * half : 192 + 48 * half] = part[48:96]
            to_rt[lev, 32 + 16 * half : 48 + 16 * half] = part[96:112]
            to_dr[lev, 32 + 16 * half : 48 + 16 * half] = part[112:128]


def place_kernel(keep_t, keep_m, rt, dn, dr, m_place, m_pm, grad_tokens, merged):
    def halves(ref, lev, start, count):
        return jnp.concatenate([ref[lev, start : start + count], ref[lev, start + count : start + 2 * count]], axis=1)

    for lev in range(4):
        low = keep_t[lev].astype(F32) + nn(m_place[...], rt[lev, 0:32])
        top = dn[lev, 0:144].astype(F32) + nn(m_place[...], dr[lev, 0:32])
        grad_tokens[lev, 0:144] = top.astype(BF16)
        grad_tokens[lev, 144:288] = low.astype(BF16)
    src = [keep_m[lev] for lev in range(4)]
    src += [halves(dn, lev, 144, 48) for lev in range(4)]
    src += [halves(rt, lev, 32, 16) for lev in range(4)]
    src += [halves(dr, lev, 32, 16) for lev in range(4)]
    got = nn(m_pm[...], jnp.concatenate(src, axis=0)).astype(BF16)
    for i in range(72):
        merged[i] = got[4 * i : 4 * i + 4]


def add_kernel(got, out, *, lats):
    total = jnp.sum(got[:, 0:CHUNK].astype(F32), axis=0).astype(BF16)
    lons = got.shape[0] // lats
    for b in range(lats):
        band = got[b, CHUNK:ROWS].astype(F32)
        for a in range(1, lons):
            band = band + got[a * lats + b, CHUNK:ROWS].astype(F32)
        band = band.astype(BF16)
        for a in range(lons):
            out[a * lats + b, 0:CHUNK] = total
            out[a * lats + b, CHUNK:ROWS] = band


def final_kernel(buf, gqkv, gproj, gfc1, gfc2t, gmerge, gbias, *, scale, bias_scale):
    def tile(base, t):
        return jnp.concatenate([buf[base + 4 * t + c, 0:CHUNK] for c in range(4)], axis=0).astype(F32) * scale

    for t in range(6):
        gfc1[:, t * 128 : t * 128 + 128] = tile(0, t)
        gfc2t[:, t * 128 : t * 128 + 128] = tile(24, t)
    for k in range(16):
        for t in range(3):
            part = buf[48 + k * 3 + t, 0:CHUNK].astype(F32) * scale
            gmerge[k * CHUNK : (k + 1) * CHUNK, t * 128 : t * 128 + 128] = part
    both = jnp.concatenate([tile(96, t) for t in range(6)], axis=1)
    gqkv[...] = both[:, 0:576]
    gproj[...] = both[:, 576:768]
    for z in range(2):
        for t in range(7):
            part = jnp.concatenate([buf[(z * 7 + t) * 9 + c, CHUNK:ROWS] for c in range(9)], axis=0)
            part = part.astype(F32).T * bias_scale
            end = min(t * 128 + 128, HQ)
            gbias[z, t * 128 : end] = part[0 : end - t * 128]


def call(kernel, outs, scratch=(), flops=10**7, size=10**6, **more):
    return pl.pallas_call(
        kernel,
        out_shape=outs,
        **more,
        scratch_shapes=list(scratch),
        compiler_params=pltpu.CompilerParams(vmem_limit_bytes=58 * 2**20),
        cost_estimate=pl.CostEstimate(flops=flops, bytes_accessed=size, transcendentals=0),
    )


def shape(*dims, kind=BF16):
    return jax.ShapeDtypeStruct(dims, kind)


def first_call():
    return call(
        first_kernel,
        (
            shape(N_CHUNK, ROWS, 128),
            shape(320, MG),
            shape(8, WT, D),
            shape(8, WT, D),
            shape(8, WT, HQ),
            shape(8, WT, D),
            shape(8, WT, D),
        ),
        [
            pltpu.VMEM((3, D, D), BF16),
            pltpu.VMEM((3, D, D), BF16),
            pltpu.VMEM((2, WT, HQ), F32),
            pltpu.VMEM((2, HQ, 128), F32),
            pltpu.VMEM((2, HQ, 128), F32),
            pltpu.VMEM((12, WT, D), F32),
            pltpu.VMEM((2, 2, 32, D), BF16),
            pltpu.VMEM((4, 320, D), BF16),
            pltpu.VMEM((4, 320, D), BF16),
            pltpu.VMEM((4, 320, FF), BF16),
            pltpu.VMEM((4, 320, FF), F32),
            pltpu.VMEM((4, 320, D), BF16),
            pltpu.VMEM((4, 320, D), BF16),
            pltpu.VMEM((8, WT, D), F32),
            pltpu.VMEM((320, MG), BF16),
        ],
        flops=2 * 10**10,
        size=10**7,
    )


def second_call():
    whole = pl.BlockSpec(memory_space=pltpu.VMEM)
    held = pl.BlockSpec(memory_space=pl.ANY)
    return call(
        second_kernel,
        (shape(N_CHUNK, ROWS, 128), shape(3, 8, WT, D)),
        [
            pltpu.VMEM((3, D, D), BF16),
            pltpu.VMEM((3, D, D), BF16),
            pltpu.VMEM((2, WT, HQ), F32),
            pltpu.VMEM((32, CHUNK, 128), BF16),
            pltpu.VMEM((N_CHUNK, 16, 128), BF16),
            pltpu.SemaphoreType.DMA((2,)),
        ],
        flops=10**10,
        size=10**7,
        in_specs=[held] + [whole] * 9,
        out_specs=(held, whole),
        input_output_aliases={0: 0},
    )


def third_call():
    return call(
        third_kernel,
        (shape(4, 144, D), shape(4, 48, MG), shape(4, 64, D), shape(4, 240, D), shape(4, 64, D)),
        [pltpu.VMEM((8, WT, D), F32)],
        flops=10**10,
        size=10**7,
    )


def body(tokens, gain_one, w_qkv, w_proj, bias_table, gain_two, w_fc1, w_fc2, gain_merge, w_merge, cotangent):
    lat_count = lax.axis_size("lat")
    lon_count = lax.axis_size("lon")
    count = lat_count * lon_count
    bottom = (lax.axis_index("lat") == lat_count - 1).astype(jnp.int32).reshape(1, 1)
    flat = tokens.reshape(4, 288, D)
    both = ("lon", "lat")

    def move(block, lon_step, lat_step):
        route = []
        for a in range(lon_count):
            for b in range(lat_count):
                to = (a + lon_step) % lon_count * lat_count + (b + lat_step) % lat_count
                route.append((a * lat_count + b, to))
        return lax.ppermute(block, both, route)

    dn, rt, lf, dr, dl, cot = call(
        pack_kernel,
        (
            shape(4, 240, D),
            shape(4, 96, D),
            shape(4, 32, D),
            shape(4, 96, D),
            shape(4, 32, D),
            shape(4, 48, MG),
        ),
        [pltpu.VMEM((288, MG), F32)],
    )(flat, cotangent.transpose(1, 2, 0, 3).reshape(72, 4, MG), pack_map(), pack_cot_map())
    dn = move(dn, 0, -1)
    rt = move(rt, -1, 0)
    lf = move(lf, 1, 0)
    dr = move(dr, -1, -1)
    dl = move(dl, 1, -1)

    head, headt, sidem, fold = head_mask(), head_mask().T, side_mask(), fold_map()
    g1 = gain_one.reshape(1, D)
    grads, merged, tok8, xn, prob, mixed, datt = first_call()(
        bottom, flat, dn, rt, lf, dr, dl, cot, bias_table.reshape(2, HQ, WT),
        g1, w_qkv, w_proj, gain_two.reshape(1, D), w_fc1, w_fc2.T, gain_merge.reshape(1, FF), w_merge,
        window_map(), cot_map(), quad_map(), back_map(), head, headt, fold, sidem, sidem.T, side_fold(),
        jnp.stack([side_pick(5, False), side_pick(0, False)]), jnp.stack([side_pick(5, True), side_pick(0, True)]),
    )
    grads, dqkv = second_call()(grads, xn, prob, mixed, datt, w_qkv, w_proj, head, headt, fold)
    keep_t, keep_m, rt, dn, dr = third_call()(tok8, datt, dqkv, merged, g1, w_qkv, out_map(), merged_map())
    grads = lax.all_to_all(grads, both, 0, 0)
    rt = move(rt, 1, 0)
    dn = move(dn, 0, 1)
    dr = move(dr, 1, 1)
    grads, rt, dn, dr = lax.optimization_barrier((grads, rt, dn, dr))
    grads = call(functools.partial(add_kernel, lats=lat_count), shape(N_CHUNK, ROWS, 128))(grads)
    grads = lax.all_to_all(grads, both, 0, 0)
    grad_tokens, merged = call(place_kernel, (shape(4, 288, D), shape(72, 4, MG)))(
        keep_t, keep_m, rt, dn, dr, place_map(), place_merged_map()
    )
    grads, grad_tokens, merged = lax.optimization_barrier((grads, grad_tokens, merged))
    gqkv, gproj, gfc1, gfc2t, gmerge, gbias = call(
        functools.partial(
            final_kernel, scale=(1152 * count) ** (-0.5), bias_scale=WT * (4 * lon_count) ** (-0.5)
        ),
        (
            shape(D, 3 * D, kind=F32),
            shape(D, D, kind=F32),
            shape(D, FF, kind=F32),
            shape(D, FF, kind=F32),
            shape(FF, MG, kind=F32),
            shape(2, HQ, WT, kind=F32),
        ),
    )(grads)
    return (
        merged.reshape(6, 12, 4, MG).transpose(2, 0, 1, 3),
        grad_tokens.reshape(4, 12, 24, D),
        gqkv,
        gproj,
        gfc1,
        gfc2t.T,
        gmerge,
        gbias.reshape(1, 2, HEADS, WT, WT),
    )


def solution(mesh):
    placed = (
        P(None, "lat", "lon", None),
        P(),
        P(),
        P(),
        P("lat", None, None, None, None),
        P(),
        P(),
        P(),
        P(),
        P(),
        P(None, "lat", "lon", None),
    )
    return jax.shard_map(
        body,
        mesh=mesh,
        in_specs=placed,
        out_specs=(
            P(None, "lat", "lon", None),
            P(None, "lat", "lon", None),
            P(),
            P(),
            P(),
            P(),
            P(),
            P("lat", None, None, None, None),
        ),
        check_vma=False,
    )
```

```python
import functools

import jax
import jax.numpy as jnp
import numpy as np
from jax import lax
from jax.experimental import pallas as pl
from jax.experimental.pallas import tpu as pltpu
from jax.sharding import PartitionSpec as P

F32 = jnp.float32
BF16 = jnp.bfloat16
EPS = 1e-05
D = 192
HEADS = 6
HD = 32
WT = 144
HQ = HEADS * WT
FF = 768
MG = 384
SCALE = HD ** (-0.5)
OFF = -1e30
SCALAR = pl.BlockSpec(memory_space=pltpu.SMEM)
WHOLE = pl.BlockSpec(memory_space=pltpu.VMEM)
LAT = ("chip", "core")
GROUP = 8
PEERS = 64
FIRST = 40
SECOND = 48
ROWS = FIRST + SECOND
HALF = PEERS * FIRST
BIAS_AT = 960


def one_hot(shape, pairs):
    table = np.zeros(shape, np.float32)
    for row, col in pairs:
        table[row, col] = 1.0
    return jnp.asarray(table, BF16)


def pack_map():
    pairs = [(r * 9 + c, r * 24 + c) for r in range(6) for c in range(9)]
    pairs += [(56 + r * 3 + c, r * 24 + 21 + c) for r in range(6) for c in range(3)]
    return one_hot((80, 144), pairs)


def pack_cot_map():
    pairs = []
    for lev in range(4):
        for r in range(3):
            for c in range(12):
                pairs.append((lev * 96 + r * 16 + c, ((3 + r) * 12 + c) * 4 + lev))
                pairs.append((lev * 96 + 48 + r * 16 + c, (r * 12 + c) * 4 + lev))
            for c in range(2):
                pairs.append((384 + lev * 6 + r * 2 + c, ((3 + r) * 12 + c) * 4 + lev))
                pairs.append((408 + lev * 6 + r * 2 + c, (r * 12 + c) * 4 + lev))
    return one_hot((432, 288), pairs)


def window_map():
    pairs = []
    for win in range(6):
        for row in range(12):
            for c in range(6):
                e, r = 6 * win + c, row % 6
                upper = row < 6
                if e < 3:
                    src = (344 if upper else 424) + r * 3 + e
                elif e < 27:
                    src = (0 if upper else 144) + r * 24 + e - 3
                else:
                    src = (288 if upper else 368) + r * 9 + e - 27
                pairs.append((win * 72 + row * 6 + c, src))
    return one_hot((432, 448), pairs)


def cot_map():
    pairs = []
    for lev in range(4):
        for r in range(6):
            for p in range(13):
                if p < 11:
                    src = lev * 96 + r * 16 + p + 1
                else:
                    src = (384 if r < 3 else 408) + lev * 6 + r % 3 * 2 + p - 11
                pairs.append((lev * 80 + r * 13 + p, src))
    return one_hot((320, 432), pairs)


def quad_pairs():
    pairs = []
    for ro in range(2):
        for co in range(2):
            for pr in range(6):
                for p in range(13):
                    row, e = 2 * pr + ro, 5 + 2 * p + co
                    if e == 5:
                        src = 288 + row
                    elif e == 30:
                        src = 304 + row
                    else:
                        src = (e - 6) // 6 * 72 + row * 6 + (e - 6) % 6
                    pairs.append(((2 * ro + co) * 80 + pr * 13 + p, src))
    return pairs


def quad_map():
    return one_hot((320, 320), quad_pairs())


def back_map():
    return one_hot((288, 320), [(s, d) for d, s in quad_pairs() if s < 288])


def out_map():
    pairs = []
    for row in range(12):
        for e in range(24):
            src = e // 6 * 72 + row * 6 + e % 6
            r = row % 6
            if e < 21:
                dst = (0 if row < 6 else 144) + r * 24 + e + 3
            else:
                dst = (288 if row < 6 else 320) + r * 3 + e - 21
            pairs.append((dst, src))
    return one_hot((352, 288), pairs)


def merged_map():
    pairs = []
    for r in range(6):
        for p in range(11):
            pairs.append(((0 if r < 3 else 48) + r % 3 * 16 + p + 1, r * 13 + p))
        pairs.append(((96 if r < 3 else 112) + r % 3, r * 13 + 11))
    return one_hot((128, 80), pairs)


def place_map():
    return one_hot((144, 32), [(r * 24 + c, r * 3 + c) for r in range(6) for c in range(3)])


def place_merged_map():
    pairs = []
    for lev in range(4):
        for r in range(6):
            for c in range(12):
                if c:
                    src = (192 if r < 3 else 0) + lev * 48 + r % 3 * 16 + c
                else:
                    src = (448 if r < 3 else 384) + lev * 16 + r % 3
                pairs.append(((r * 12 + c) * 4 + lev, src))
    return one_hot((288, 512), pairs)


def head_mask():
    return one_hot((HQ, D), [(h * WT + q, h * HD + c) for h in range(HEADS) for q in range(WT) for c in range(HD)])


def fold_map():
    return one_hot((WT, HQ), [(q, h * WT + q) for h in range(HEADS) for q in range(WT)])


def side_mask():
    return one_hot((WT, D), [(h * 24 + q, h * HD + c) for h in range(HEADS) for q in range(24) for c in range(HD)])


def side_fold():
    pairs = [(li * 16 + r, h * 24 + li * 12 + r) for h in range(HEADS) for li in range(2) for r in range(12)]
    return one_hot((32, WT), pairs)


def side_pick(col, padded):
    step, heads = (16, 1) if padded else (12, HEADS)
    pairs = [
        (h * 2 * step + li * step + r, li * 72 + r * 6 + col)
        for h in range(heads)
        for li in range(2)
        for r in range(12)
    ]
    return one_hot((2 * step * heads, WT), pairs)


def nn(a, b):
    return lax.dot_general(a, b, (((1,), (0,)), ((), ())), preferred_element_type=F32)


def nt(a, b):
    return lax.dot_general(a, b, (((1,), (1,)), ((), ())), preferred_element_type=F32)


def tn(a, b):
    return lax.dot_general(a, b, (((0,), (0,)), ((), ())), preferred_element_type=F32)


def norm_parts(values):
    center = values - jnp.mean(values, axis=-1, keepdims=True)
    rstd = lax.rsqrt(jnp.mean(center * center, axis=-1, keepdims=True) + EPS)
    return center * rstd, rstd


def norm_back(hat, rstd, gain, upstream):
    g = upstream * gain
    return rstd * (g - jnp.mean(g, axis=-1, keepdims=True) - hat * jnp.mean(g * hat, axis=-1, keepdims=True))


LEVEL_AT = ((1, 1), (0, 0), (0, 1), (1, 0))


def pack_kernel(tok, cot, pmap, cmap, dn, rt, lf, dr, dl, here, rows, wide, narrow):
    for i in range(72):
        rows[4 * i : 4 * i + 4] = cot[i].astype(F32)
    c = nn(cmap[...], rows[...].astype(BF16))
    wide[...] = jnp.zeros_like(wide)
    narrow[...] = jnp.zeros_like(narrow)
    for lev in range(4):
        top = tok[lev, 0:144]
        dn[lev, 0:144] = top
        for side, block in enumerate((tok[lev, 144:288], top)):
            got = nn(pmap[...], block)
            wide[side, lev * 54 : lev * 54 + 54] = got[0:54]
            narrow[side, lev * 18 : lev * 18 + 18] = got[56:74]
        here[lev] = c[lev * 96 : lev * 96 + 48].astype(BF16)
        part = c[lev * 96 + 48 : lev * 96 + 96].astype(BF16)
        dn[lev, 144:192] = part[:, 0:D]
        dn[lev, 192:240] = part[:, D : 2 * D]
    for side in range(2):
        part = c[384 + 24 * side : 408 + 24 * side]
        wide[side, 216:240] = part[:, 0:D]
        wide[side, 240:264] = part[:, D : 2 * D]
    rt[...] = wide[0].astype(BF16)
    dr[...] = wide[1].astype(BF16)
    lf[...] = narrow[0].astype(BF16)
    dl[...] = narrow[1].astype(BF16)


def label(pos, z, bottom):
    row = ((pos % 72 >= 36) & bottom).astype(jnp.int32)
    return row + (2 * (pos // 72).astype(jnp.int32) if z == 1 else 0)


def split_weights(wqkv, w3, wt3):
    eye = (lax.broadcasted_iota(jnp.int32, (D, D), 0) == lax.broadcasted_iota(jnp.int32, (D, D), 1)).astype(BF16)
    for part in range(3):
        w = wqkv[:, part * D : (part + 1) * D]
        w3[part] = w
        wt3[part] = nt(eye, w).astype(BF16)


def first_kernel(
    core_ref, bottom_ref, own, dn, rt, lf, dr, dl, cot, bias, gain_one, wqkv, wproj, gain_two, wfc1, wfc2t, gain_merge, wmerge,
    m_win, m_cot, m_quad, m_back, m_head, m_headt, m_fold, m_side, m_sidet, m_sfold, m_pick, m_there,
    stay, leave, merged, tok8, xn, prob, dout,
    grads, w3, wt3, bias_t, low_cols, high_cols, halo, mixed, tok, side, resq, mlpin, act, dgel, blk, dresq, resw, cotq,
):
    split_weights(wqkv, w3, wt3)
    bottom = bottom_ref[0, 0] > 0
    lane = lax.broadcasted_iota(jnp.int32, (1, HQ), 1) % WT
    row = lax.broadcasted_iota(jnp.int32, (WT, 1), 0)
    for z in range(2):
        bias_t[z] = jnp.where(label(row, z, bottom) != label(lane, z, bottom), OFF, bias[z].T)
        low_cols[z] = bias[z, :, 0:128]
        high_cols[z, :, 0 : WT - 128] = bias[z, :, 128:WT]

    halo[...] = jnp.zeros_like(halo)
    rt_, lf_, dr_, dl_ = (ref[...].astype(F32) for ref in (rt, lf, dr, dl))
    for lev in range(4):
        z, li = LEVEL_AT[lev]
        halo[0:54] = rt_[lev * 54 : lev * 54 + 54]
        halo[56:74] = lf_[lev * 18 : lev * 18 + 18]
        halo[80:134] = dr_[lev * 54 : lev * 54 + 54]
        halo[136:154] = dl_[lev * 18 : lev * 18 + 18]
        src = jnp.concatenate([own[lev, 144:288], dn[lev, 0:144], halo[...].astype(BF16)], axis=0)
        got = nn(m_win[...], src)
        for win in range(6):
            tok[z * 6 + win, li * 72 : li * 72 + 72] = got[win * 72 : win * 72 + 72]

    g1 = gain_one[...]

    def forward(i, carry):
        ws = [i * GROUP + n for n in range(GROUP)]
        zs = [w // 4 for w in ws]
        ts = [tok[z * 6 + w % 4 + 1] for w, z in zip(ws, zs)]
        xs = [(norm_parts(t)[0] * g1).astype(BF16) for t in ts]
        for w, t, x in zip(ws, ts, xs):
            tok8[w] = t.astype(BF16)
            xn[w] = x
        qs = [nn(x, w3[0]).astype(BF16) for x in xs]
        ks = [nn(x, w3[1]).astype(BF16) for x in xs]
        vts = [nt(wt3[2], x).astype(BF16) for x in xs]
        ss = [nt(k, jnp.concatenate([q] * HEADS, axis=0) * m_head[...]) for q, k in zip(qs, ks)]
        ps = []
        for w, z, score in zip(ws, zs, ss):
            e = jnp.exp(score * SCALE + bias_t[z])
            p = (e * (1.0 / jnp.sum(e, axis=0, keepdims=True))).astype(BF16)
            prob[w] = p
            ps.append(p)
        fulls = [nn(vt, p).astype(BF16) * m_headt[...] for vt, p in zip(vts, ps)]
        mxs = [nt(m_fold[...], full).astype(BF16) for full in fulls]
        for w, t, mx in zip(ws, ts, mxs):
            mixed[w] = mx
            att = nn(mx, wproj[...]).astype(BF16)
            resw[w] = (t + att.astype(F32)).astype(BF16).astype(F32)
        return carry

    lax.fori_loop(0, 8 // GROUP, forward, 0)

    lane = lax.broadcasted_iota(jnp.int32, (1, WT), 1) % 24
    lane = lane // 12 * 72 + lane % 12 * 6
    beside = [(n, z) for n in range(2) for z in range(2)]
    ts = [tok[z * 6 + 5 * n] for n, z in beside]
    xs = [(norm_parts(t)[0] * g1).astype(BF16) for t in ts]
    qs = [nn(x, w3[0]).astype(BF16) for x in xs]
    ks = [nn(x, w3[1]).astype(BF16) for x in xs]
    vts = [nt(wt3[2], x).astype(BF16) for x in xs]
    ss = [nt(k, nn(m_pick[n], q).astype(BF16) * m_side[...]) for q, k, (n, z) in zip(qs, ks, beside)]
    ps = []
    for score, (n, z) in zip(ss, beside):
        every = pl.ds(5 - 5 * n, WT, stride=6)
        table = jnp.concatenate([low_cols[z, every, :], high_cols[z, every, :][:, 0 : WT - 128]], axis=1).T
        table = jnp.where(label(row, z, bottom) != label(lane, z, bottom), OFF, table)
        e = jnp.exp(score * SCALE + table)
        ps.append((e * (1.0 / jnp.sum(e, axis=0, keepdims=True))).astype(BF16))
    fulls = [nn(vt, p).astype(BF16) * m_sidet[...] for vt, p in zip(vts, ps)]
    mxs = [nt(m_sfold[...], full).astype(BF16) for full in fulls]
    for t, mx, (n, z) in zip(ts, mxs, beside):
        att = nn(mx, wproj[...]).astype(BF16)
        there = nn(m_there[n], t.astype(BF16))
        side[n, z] = (there + att.astype(F32)).astype(BF16)

    for lev in range(4):
        z, li = LEVEL_AT[lev]
        src = jnp.concatenate([resw[z * 4 + win, li * 72 : li * 72 + 72] for win in range(4)], axis=0).astype(BF16)
        src = jnp.concatenate([src, side[0, z, li * 16 : li * 16 + 16], side[1, z, li * 16 : li * 16 + 16]], axis=0)
        got = nn(m_quad[...], src).astype(BF16)
        for k in range(4):
            resq[k, lev * 80 : lev * 80 + 80] = got[k * 80 : k * 80 + 80]

    src = []
    for lev in range(4):
        src += [cot[lev], jnp.concatenate([dn[lev, 144:192], dn[lev, 192:240]], axis=1)]
    for block in (rt_, dr_):
        src.append(jnp.concatenate([block[216:240], block[240:264]], axis=1))
    src = jnp.concatenate(src[:8] + [jnp.concatenate(src[8:], axis=0).astype(BF16)], axis=0)
    cotq[...] = nn(m_cot[...], src).astype(BF16)

    g2 = gain_two[...]
    inner = np.float32(np.sqrt(2 / np.pi))

    def feed(k, carry):
        res = resq[k].astype(F32)
        hat, _ = norm_parts(res)
        mi = (hat * g2).astype(BF16)
        mlpin[k] = mi
        pre = nn(mi, wfc1[...])
        sq = pre * pre
        t = jnp.tanh(pre * (inner + (inner * 0.044715) * sq))
        half = 0.5 + 0.5 * t
        full = pre * half
        a = full.astype(BF16)
        act[k] = a
        dgel[k] = half + full * (1.0 - half) * (2 * inner + (6 * inner * 0.044715) * sq)
        blk[k] = (res + nt(a, wfc2t[...])).astype(BF16)
        return carry

    lax.fori_loop(0, 4, feed, 0)

    total = 0.0
    for k in range(4):
        total = total + jnp.sum(blk[k].astype(F32), axis=-1, keepdims=True)
    mean = total * (1.0 / 768)
    total = 0.0
    for k in range(4):
        center = blk[k].astype(F32) - mean
        total = total + jnp.sum(center * center, axis=-1, keepdims=True)
    rstd = lax.rsqrt(total * (1.0 / 768) + EPS)
    cq = cotq[...]
    pair = lax.broadcasted_iota(jnp.int32, (320, MG), 0) % 80 % 13
    cq_own = jnp.where(pair < 12, cq.astype(F32), 0.0).astype(BF16)
    out = 0.0
    sum_a = 0.0
    sum_b = 0.0
    for k in range(4):
        gm = gain_merge[:, k * D : k * D + D]
        hat = (blk[k].astype(F32) - mean) * rstd
        mn = (hat * gm).astype(BF16)
        wm = wmerge[k * D : k * D + D]
        out = out + nn(mn, wm)
        gmerge = tn(mn, cq_own).astype(BF16)
        for t in range(3):
            at = t * 768 + k * D
            grads[1, at : at + D] = gmerge[:, t * 128 : t * 128 + 128]
        g = nt(cq, wm) * gm
        sum_a = sum_a + jnp.sum(g, axis=-1, keepdims=True)
        sum_b = sum_b + jnp.sum(g * hat, axis=-1, keepdims=True)
    merged[...] = out.astype(BF16)
    sum_a = sum_a * (1.0 / 768)
    sum_b = sum_b * (1.0 / 768)
    pair = lax.broadcasted_iota(jnp.int32, (320, D), 0) % 80 % 13
    fc1 = 0.0
    fc2 = 0.0
    for k in range(4):
        wm = wmerge[k * D : k * D + D]
        hat = (blk[k].astype(F32) - mean) * rstd
        g = nt(cq, wm) * gain_merge[:, k * D : k * D + D]
        d = rstd * (g - sum_a - hat * sum_b)
        d = jnp.where(pair == (0 if k % 2 == 0 else 12), 0.0, d)
        db = d.astype(BF16)
        dpre = (nn(db, wfc2t[...]) * dgel[k]).astype(BF16)
        fc2 = fc2 + tn(db, act[k])
        fc1 = fc1 + tn(mlpin[k], dpre)
        dmlp = nt(dpre, wfc1[...])
        hat2, rstd2 = norm_parts(resq[k].astype(F32))
        dresq[k] = (db.astype(F32) + norm_back(hat2, rstd2, g2, dmlp)).astype(BF16)
    for base, value in ((0, fc1.astype(BF16)), (1152, fc2.astype(BF16))):
        for t in range(6):
            grads[0, base + t * D : base + t * D + D] = value[:, t * 128 : t * 128 + 128]

    for lev in range(4):
        z, li = LEVEL_AT[lev]
        src = jnp.concatenate([dresq[k, lev * 80 : lev * 80 + 80] for k in range(4)], axis=0)
        got = nn(m_back[...], src)
        for win in range(4):
            resw[z * 4 + win, li * 72 : li * 72 + 72] = got[win * 72 : win * 72 + 72]
    dout[...] = resw[...].astype(BF16)
    grads[:, 2304:HALF] = jnp.zeros((2, HALF - 2304, 128), BF16)
    gproj = tn(mixed[...].reshape(8 * WT, D), dout[...].reshape(8 * WT, D)).astype(BF16)
    grads[0, 2304 : 2304 + D] = gproj[:, 0:128]
    grads[1, 2304 : 2304 + D, 0:64] = gproj[:, 128:192]
    core = core_ref[0, 0]
    stay[...] = grads[core]
    leave[...] = grads[1 - core]


def second_kernel(
    xn, prob, datt, wqkv, wproj, m_head, m_headt, m_fold,
    grads, dqkv,
    w3, wt3, gb,
):
    split_weights(wqkv, w3, wt3)
    gb[...] = jnp.zeros_like(gb)

    def backward(i, carry):
        ws = [i * GROUP + n for n in range(GROUP)]
        xs = [xn[w] for w in ws]
        ups = [datt[w] for w in ws]
        qs = [nn(x, w3[0]).astype(BF16) for x in xs]
        vs = [nn(x, w3[2]).astype(BF16) for x in xs]
        kts = [nt(wt3[1], x).astype(BF16) for x in xs]
        dms = [nt(up, wproj[...]).astype(BF16) for up in ups]
        dmbds = [jnp.concatenate([dm] * HEADS, axis=0) * m_head[...] for dm in dms]
        dps = [nt(v, dmbd) for v, dmbd in zip(vs, dmbds)]
        dsbs = []
        for w, dp in zip(ws, dps):
            p = prob[w].astype(F32)
            ds = p * (dp - jnp.sum(dp * p, axis=0, keepdims=True))
            gb[w // 4] += ds
            dsbs.append((ds * SCALE).astype(BF16))
        for w, dmbd in zip(ws, dmbds):
            dqkv[2, w] = nn(prob[w], dmbd).astype(BF16)
        qbds = [jnp.concatenate([q] * HEADS, axis=0) * m_head[...] for q in qs]
        for w, dsb, qbd in zip(ws, dsbs, qbds):
            dqkv[1, w] = nn(dsb, qbd).astype(BF16)
        fulls = [nn(kt, dsb).astype(BF16) * m_headt[...] for kt, dsb in zip(kts, dsbs)]
        for w, full in zip(ws, fulls):
            dqkv[0, w] = nt(m_fold[...], full).astype(BF16)
        return carry

    lax.fori_loop(0, 8 // GROUP, backward, 0)

    xs = xn[...].reshape(8 * WT, D)
    parts = [tn(xs, dqkv[part].reshape(8 * WT, D)) for part in range(3)]
    value = jnp.concatenate(parts, axis=1).astype(BF16)
    for t in range(4):
        grads[t * D : t * D + D] = value[:, t * 128 : t * 128 + 128]
    grads[768:960, 0:64] = value[:, 512:576]
    grads[768:960, 64:128] = jnp.zeros((D, 64), BF16)
    for z in range(2):
        total = gb[z].astype(BF16)
        for t in range(7):
            tile = total[:, t * 128 : min(t * 128 + 128, HQ)]
            if t == 6:
                tile = jnp.concatenate([tile, jnp.zeros((WT, 896 - HQ), BF16)], axis=1)
            at = BIAS_AT + (z * 7 + t) * WT
            grads[at : at + WT] = tile
    grads[BIAS_AT + 14 * WT :] = jnp.zeros((PEERS * SECOND - BIAS_AT - 14 * WT, 128), BF16)


def third_kernel(
    tok8, datt, dqkv, merged, gain_one, wqkv, m_out, m_merged,
    keep_t, keep_m, to_rt, to_dn, to_dr,
    gt,
):
    g1 = gain_one[...]
    ws = [wqkv[:, part * D : (part + 1) * D] for part in range(3)]
    for w in range(8):
        dnorm = (nt(dqkv[0, w], ws[0]) + nt(dqkv[1, w], ws[1]) + nt(dqkv[2, w], ws[2])).astype(BF16).astype(F32)
        hat, rstd = norm_parts(tok8[w].astype(F32))
        gt[w] = (datt[w].astype(F32) + norm_back(hat, rstd, g1, dnorm)).astype(BF16).astype(F32)

    for lev in range(4):
        z, li = LEVEL_AT[lev]
        src = jnp.concatenate([gt[z * 4 + win, li * 72 : li * 72 + 72] for win in range(4)], axis=0).astype(BF16)
        got = nn(m_out[...], src).astype(BF16)
        keep_t[lev] = got[0:144]
        to_dn[lev, 0:144] = got[144:288]
        to_rt[lev, 0:32] = got[288:320]
        to_dr[lev, 0:32] = got[320:352]
        got = nn(m_merged[...], merged[lev * 80 : lev * 80 + 80]).astype(BF16)
        keep_m[lev] = got[0:48]
        for half in range(2):
            part = got[:, half * D : half * D + D]
            to_dn[lev, 144 + 48 * half : 192 + 48 * half] = part[48:96]
            to_rt[lev, 32 + 16 * half : 48 + 16 * half] = part[96:112]
            to_dr[lev, 32 + 16 * half : 48 + 16 * half] = part[112:128]


def place_kernel(keep_t, keep_m, rt, dn, dr, m_place, m_pm, grad_tokens, merged):
    def halves(ref, lev, start, count):
        return jnp.concatenate([ref[lev, start : start + count], ref[lev, start + count : start + 2 * count]], axis=1)

    for lev in range(4):
        low = keep_t[lev].astype(F32) + nn(m_place[...], rt[lev, 0:32])
        top = dn[lev, 0:144].astype(F32) + nn(m_place[...], dr[lev, 0:32])
        grad_tokens[lev, 0:144] = top.astype(BF16)
        grad_tokens[lev, 144:288] = low.astype(BF16)
    src = [keep_m[lev] for lev in range(4)]
    src += [halves(dn, lev, 144, 48) for lev in range(4)]
    src += [halves(rt, lev, 32, 16) for lev in range(4)]
    src += [halves(dr, lev, 32, 16) for lev in range(4)]
    got = nn(m_pm[...], jnp.concatenate(src, axis=0)).astype(BF16)
    for i in range(72):
        merged[i] = got[4 * i : 4 * i + 4]


def add_kernel(is_weight, got, out, *, bands):
    count = got.shape[0]
    mine = got[0, 0:FIRST].astype(F32)
    for n in range(1, count):
        mine = mine + got[n, 0:FIRST].astype(F32)
    mine = mine.astype(BF16)
    total = 0.0
    parts = []
    for b in range(bands):
        part = got[b, FIRST:ROWS].astype(F32)
        for n in range(b + bands, count, bands):
            part = part + got[n, FIRST:ROWS].astype(F32)
        parts.append(part)
        total = total + part
    flag = is_weight[0, 0] > 0
    for b in range(bands):
        part = jnp.where(flag, total, parts[b]).astype(BF16)
        for n in range(b, count, bands):
            out[n, 0:FIRST] = mine
            out[n, FIRST:ROWS] = part


def pieces(start, count, size):
    while count:
        chunk, off = start // size, start % size
        take = min(count, size - off)
        yield chunk, off, take
        start, count = start + take, count - take


def bias_kernel(buf, gbias, *, scale):
    def rows(start, count):
        got = [buf[c, FIRST + off : FIRST + off + n].astype(F32) for c, off, n in pieces(start, count, SECOND)]
        return jnp.concatenate(got, axis=0)

    for z in range(2):
        for t in range(7):
            part = rows(BIAS_AT + (z * 7 + t) * WT, WT).T * scale
            end = min(t * 128 + 128, HQ)
            gbias[z, t * 128 : end] = part[0 : end - t * 128]


def final_kernel(core_ref, buf, oth, gqkv, gproj, gfc1, gfc2t, gmerge, *, scale):
    here = core_ref[0, 0]

    def first(half, start, count):
        got = []
        for c, off, n in pieces(start, count, FIRST):
            got.append(jnp.where(here == half, buf[c, off : off + n], oth[c, off : off + n]).astype(F32))
        return jnp.concatenate(got, axis=0) * scale

    def second(start, count):
        got = []
        for c, off, n in pieces(start, count, SECOND):
            at = FIRST + off
            got.append(buf[c, at : at + n].astype(F32) + oth[c, at : at + n].astype(F32))
        return jnp.concatenate(got, axis=0) * scale

    for t in range(6):
        gfc1[:, t * 128 : t * 128 + 128] = first(0, t * D, D)
        gfc2t[:, t * 128 : t * 128 + 128] = first(0, 1152 + t * D, D)
    for t in range(3):
        gmerge[:, t * 128 : t * 128 + 128] = first(1, t * 768, 768)
    gproj[:, 0:128] = first(0, 2304, D)
    gproj[:, 128:192] = first(1, 2304, D)[:, 0:64]
    for t in range(5):
        end = min(t * 128 + 128, 576)
        gqkv[:, t * 128 : end] = second(t * D, D)[:, 0 : end - t * 128]


def call(kernel, outs, scratch=(), flops=10**7, size=10**6, limit=16, **more):
    return pl.pallas_call(
        kernel,
        out_shape=outs,
        **more,
        scratch_shapes=list(scratch),
        compiler_params=pltpu.CompilerParams(vmem_limit_bytes=limit * 2**20),
        cost_estimate=pl.CostEstimate(flops=flops, bytes_accessed=size, transcendentals=0),
    )


def shape(*dims, kind=BF16):
    return jax.ShapeDtypeStruct(dims, kind)


def first_call():
    return call(
        first_kernel,
        (
            shape(HALF, 128),
            shape(HALF, 128),
            shape(320, MG),
            shape(8, WT, D),
            shape(8, WT, D),
            shape(8, WT, HQ),
            shape(8, WT, D),
        ),
        [
            pltpu.VMEM((2, HALF, 128), BF16),
            pltpu.VMEM((3, D, D), BF16),
            pltpu.VMEM((3, D, D), BF16),
            pltpu.VMEM((2, WT, HQ), F32),
            pltpu.VMEM((2, HQ, 128), F32),
            pltpu.VMEM((2, HQ, 128), F32),
            pltpu.VMEM((160, D), F32),
            pltpu.VMEM((8, WT, D), BF16),
            pltpu.VMEM((12, WT, D), F32),
            pltpu.VMEM((2, 2, 32, D), BF16),
            pltpu.VMEM((4, 320, D), BF16),
            pltpu.VMEM((4, 320, D), BF16),
            pltpu.VMEM((4, 320, FF), BF16),
            pltpu.VMEM((4, 320, FF), F32),
            pltpu.VMEM((4, 320, D), BF16),
            pltpu.VMEM((4, 320, D), BF16),
            pltpu.VMEM((8, WT, D), F32),
            pltpu.VMEM((320, MG), BF16),
        ],
        flops=2 * 10**10,
        size=10**7,
        limit=58,
    )


def second_call():
    return call(
        second_kernel,
        (shape(PEERS * SECOND, 128), shape(3, 8, WT, D)),
        [
            pltpu.VMEM((3, D, D), BF16),
            pltpu.VMEM((3, D, D), BF16),
            pltpu.VMEM((2, WT, HQ), F32),
        ],
        flops=10**10,
        size=10**7,
        limit=32,
    )


def third_call():
    return call(
        third_kernel,
        (shape(4, 144, D), shape(4, 48, MG), shape(4, 64, D), shape(4, 240, D), shape(4, 64, D)),
        [pltpu.VMEM((8, WT, D), F32)],
        flops=10**10,
        size=10**7,
    )


def body(tokens, gain_one, w_qkv, w_proj, bias_table, gain_two, w_fc1, w_fc2, gain_merge, w_merge, cotangent):
    lat_count = lax.axis_size(LAT)
    lon_count = lax.axis_size("lon")
    count = lat_count * lon_count
    peers = ("lon", "chip")
    bottom = (lax.axis_index(LAT) == lat_count - 1).astype(jnp.int32).reshape(1, 1)
    core = lax.axis_index("core").reshape(1, 1)
    flat = tokens.reshape(4, 288, D)

    def move(block, lon_step, lat_step):
        route = []
        for a in range(lon_count):
            for b in range(lat_count):
                to = (a + lon_step) % lon_count * lat_count + (b + lat_step) % lat_count
                route.append((a * lat_count + b, to))
        return lax.ppermute(block, ("lon",) + LAT, route)

    dn, rt, lf, dr, dl, cot = call(
        pack_kernel,
        (
            shape(4, 240, D),
            shape(272, D),
            shape(80, D),
            shape(272, D),
            shape(80, D),
            shape(4, 48, MG),
        ),
        [pltpu.VMEM((288, MG), F32), pltpu.VMEM((2, 272, D), F32), pltpu.VMEM((2, 80, D), F32)],
        limit=58,
    )(flat, cotangent.transpose(1, 2, 0, 3).reshape(72, 4, MG), pack_map(), pack_cot_map())
    dn = move(dn, 0, -1)
    rt = move(rt, -1, 0)
    lf = move(lf, 1, 0)
    dr = move(dr, -1, -1)
    dl = move(dl, 1, -1)

    head, headt, sidem, fold = head_mask(), head_mask().T, side_mask(), fold_map()
    g1 = gain_one.reshape(1, D)
    first, leave, merged, tok8, xn, prob, datt = first_call()(
        core, bottom, flat, dn, rt, lf, dr, dl, cot, bias_table.reshape(2, HQ, WT),
        g1, w_qkv, w_proj, gain_two.reshape(1, D), w_fc1, w_fc2.T, gain_merge.reshape(1, FF), w_merge,
        window_map(), cot_map(), quad_map(), back_map(), head, headt, fold, sidem, sidem.T, side_fold(),
        jnp.stack([side_pick(5, False), side_pick(0, False)]), jnp.stack([side_pick(5, True), side_pick(0, True)]),
    )
    arrived = lax.ppermute(leave, "core", [(0, 1), (1, 0)])
    second, dqkv = second_call()(xn, prob, datt, w_qkv, w_proj, head, headt, fold)
    arrived, second = lax.optimization_barrier((arrived, second))
    first = (first.astype(F32) + arrived.astype(F32)).astype(BF16).reshape(PEERS, FIRST, 128)
    grads = jnp.concatenate([first, second.reshape(PEERS, SECOND, 128)], axis=1)
    grads = lax.all_to_all(grads, peers, 0, 0)
    keep_t, keep_m, rt, dn, dr = third_call()(tok8, datt, dqkv, merged, g1, w_qkv, out_map(), merged_map())
    rt = move(rt, 1, 0)
    dn = move(dn, 0, 1)
    dr = move(dr, 1, 1)
    grads, rt, dn, dr = lax.optimization_barrier((grads, rt, dn, dr))
    place = lax.axis_index(peers)
    is_weight = (place < BIAS_AT // SECOND).astype(jnp.int32).reshape(1, 1)
    grads = call(
        functools.partial(add_kernel, bands=lax.axis_size("chip")), shape(PEERS, ROWS, 128), in_specs=[SCALAR, WHOLE]
    )(is_weight, grads)
    grads = lax.all_to_all(grads, peers, 0, 0)
    grad_tokens, merged = call(place_kernel, (shape(4, 288, D), shape(72, 4, MG)))(
        keep_t, keep_m, rt, dn, dr, place_map(), place_merged_map()
    )
    grads, grad_tokens, merged = lax.optimization_barrier((grads, grad_tokens, merged))
    other = lax.ppermute(grads, "core", [(0, 1), (1, 0)])
    gbias = call(
        functools.partial(bias_kernel, scale=WT * (4 * lon_count) ** (-0.5)), shape(2, HQ, WT, kind=F32)
    )(grads)
    gqkv, gproj, gfc1, gfc2t, gmerge = call(
        functools.partial(final_kernel, scale=(1152 * count) ** (-0.5)),
        (
            shape(D, 3 * D, kind=F32),
            shape(D, D, kind=F32),
            shape(D, FF, kind=F32),
            shape(D, FF, kind=F32),
            shape(FF, MG, kind=F32),
        ),
        in_specs=[SCALAR, WHOLE, WHOLE],
    )(core, grads, other)
    return (
        merged.reshape(6, 12, 4, MG).transpose(2, 0, 1, 3),
        grad_tokens.reshape(4, 12, 24, D),
        gqkv,
        gproj,
        gfc1,
        gfc2t.T,
        gmerge,
        gbias.reshape(1, 2, HEADS, WT, WT),
    )


def solution(mesh):
    lons, lats = mesh.devices.shape
    mesh = jax.sharding.Mesh(mesh.devices.reshape(lons, lats // 2, 2), ("lon",) + LAT)
    placed = (
        P(None, LAT, "lon", None),
        P(),
        P(),
        P(),
        P(LAT, None, None, None, None),
        P(),
        P(),
        P(),
        P(),
        P(),
        P(None, LAT, "lon", None),
    )
    return jax.shard_map(
        body,
        mesh=mesh,
        in_specs=placed,
        out_specs=(
            P(None, LAT, "lon", None),
            P(None, LAT, "lon", None),
            P(),
            P(),
            P(),
            P(),
            P(),
            P(LAT, None, None, None, None),
        ),
        check_vma=False,
    )
```

```python
import functools

import jax
import jax.numpy as jnp
import numpy as np
from jax import lax
from jax.experimental import pallas as pl
from jax.experimental.pallas import tpu as pltpu
from jax.sharding import PartitionSpec as P

F32 = jnp.float32
BF16 = jnp.bfloat16
EPS = 1e-05
D = 192
HEADS = 6
HD = 32
WT = 144
HQ = HEADS * WT
FF = 768
MG = 384
SCALE = HD ** (-0.5)
OFF = -1e30
SCALAR = pl.BlockSpec(memory_space=pltpu.SMEM)
WHOLE = pl.BlockSpec(memory_space=pltpu.VMEM)
LAT = ("chip", "core")
GROUP = 8
PEERS = 64
FIRST = 40
SECOND = 48
ROWS = FIRST + SECOND
HALF = PEERS * FIRST
BIAS_AT = 960


def one_hot(shape, pairs):
    table = np.zeros(shape, np.float32)
    for row, col in pairs:
        table[row, col] = 1.0
    return jnp.asarray(table, BF16)


def pack_map():
    pairs = [(r * 9 + c, r * 24 + c) for r in range(6) for c in range(9)]
    pairs += [(56 + r * 3 + c, r * 24 + 21 + c) for r in range(6) for c in range(3)]
    return one_hot((80, 144), pairs)


def pack_cot_map():
    pairs = []
    for lev in range(4):
        for r in range(3):
            for c in range(12):
                pairs.append((lev * 96 + r * 16 + c, ((3 + r) * 12 + c) * 4 + lev))
                pairs.append((lev * 96 + 48 + r * 16 + c, (r * 12 + c) * 4 + lev))
            for c in range(2):
                pairs.append((384 + lev * 6 + r * 2 + c, ((3 + r) * 12 + c) * 4 + lev))
                pairs.append((408 + lev * 6 + r * 2 + c, (r * 12 + c) * 4 + lev))
    return one_hot((432, 288), pairs)


def window_map():
    pairs = []
    for win in range(6):
        for row in range(12):
            for c in range(6):
                e, r = 6 * win + c, row % 6
                upper = row < 6
                if e < 3:
                    src = (344 if upper else 424) + r * 3 + e
                elif e < 27:
                    src = (0 if upper else 144) + r * 24 + e - 3
                else:
                    src = (288 if upper else 368) + r * 9 + e - 27
                pairs.append((win * 72 + row * 6 + c, src))
    return one_hot((432, 448), pairs)


def cot_map():
    pairs = []
    for lev in range(4):
        for r in range(6):
            for p in range(13):
                if p < 11:
                    src = lev * 96 + r * 16 + p + 1
                else:
                    src = (384 if r < 3 else 408) + lev * 6 + r % 3 * 2 + p - 11
                pairs.append((lev * 80 + r * 13 + p, src))
    return one_hot((320, 432), pairs)


def quad_pairs():
    pairs = []
    for ro in range(2):
        for co in range(2):
            for pr in range(6):
                for p in range(13):
                    row, e = 2 * pr + ro, 5 + 2 * p + co
                    if e == 5:
                        src = 288 + row
                    elif e == 30:
                        src = 304 + row
                    else:
                        src = (e - 6) // 6 * 72 + row * 6 + (e - 6) % 6
                    pairs.append(((2 * ro + co) * 80 + pr * 13 + p, src))
    return pairs


def quad_map():
    return one_hot((320, 320), quad_pairs())


def back_map():
    return one_hot((288, 320), [(s, d) for d, s in quad_pairs() if s < 288])


def out_map():
    pairs = []
    for row in range(12):
        for e in range(24):
            src = e // 6 * 72 + row * 6 + e % 6
            r = row % 6
            if e < 21:
                dst = (0 if row < 6 else 144) + r * 24 + e + 3
            else:
                dst = (288 if row < 6 else 320) + r * 3 + e - 21
            pairs.append((dst, src))
    return one_hot((352, 288), pairs)


def merged_map():
    pairs = []
    for r in range(6):
        for p in range(11):
            pairs.append(((0 if r < 3 else 48) + r % 3 * 16 + p + 1, r * 13 + p))
        pairs.append(((96 if r < 3 else 112) + r % 3, r * 13 + 11))
    return one_hot((128, 80), pairs)


def place_map():
    return one_hot((144, 32), [(r * 24 + c, r * 3 + c) for r in range(6) for c in range(3)])


def place_merged_map():
    pairs = []
    for lev in range(4):
        for r in range(6):
            for c in range(12):
                if c:
                    src = (192 if r < 3 else 0) + lev * 48 + r % 3 * 16 + c
                else:
                    src = (448 if r < 3 else 384) + lev * 16 + r % 3
                pairs.append(((r * 12 + c) * 4 + lev, src))
    return one_hot((288, 512), pairs)


def head_mask():
    return one_hot((HQ, D), [(h * WT + q, h * HD + c) for h in range(HEADS) for q in range(WT) for c in range(HD)])


def side_mask():
    return one_hot((WT, D), [(h * 24 + q, h * HD + c) for h in range(HEADS) for q in range(24) for c in range(HD)])


def side_fold():
    pairs = [(li * 16 + r, h * 24 + li * 12 + r) for h in range(HEADS) for li in range(2) for r in range(12)]
    return one_hot((32, WT), pairs)


def side_pick(col, padded):
    step, heads = (16, 1) if padded else (12, HEADS)
    pairs = [
        (h * 2 * step + li * step + r, li * 72 + r * 6 + col)
        for h in range(heads)
        for li in range(2)
        for r in range(12)
    ]
    return one_hot((2 * step * heads, WT), pairs)


def nn(a, b):
    return lax.dot_general(a, b, (((1,), (0,)), ((), ())), preferred_element_type=F32)


def nt(a, b):
    return lax.dot_general(a, b, (((1,), (1,)), ((), ())), preferred_element_type=F32)


def tn(a, b):
    return lax.dot_general(a, b, (((0,), (0,)), ((), ())), preferred_element_type=F32)


def by_head(left, right):
    parts = [nn(left[h * HD : h * HD + HD], right[:, h * WT : h * WT + WT]) for h in range(HEADS)]
    return jnp.concatenate(parts, axis=0).T


def norm_parts(values):
    center = values - jnp.mean(values, axis=-1, keepdims=True)
    rstd = lax.rsqrt(jnp.mean(center * center, axis=-1, keepdims=True) + EPS)
    return center * rstd, rstd


def norm_back(hat, rstd, gain, upstream):
    g = upstream * gain
    return rstd * (g - jnp.mean(g, axis=-1, keepdims=True) - hat * jnp.mean(g * hat, axis=-1, keepdims=True))


LEVEL_AT = ((1, 1), (0, 0), (0, 1), (1, 0))


def pack_kernel(tok, cot, pmap, cmap, dn, rt, lf, dr, dl, here, rows, wide, narrow):
    for i in range(72):
        rows[4 * i : 4 * i + 4] = cot[i].astype(F32)
    c = nn(cmap[...], rows[...].astype(BF16))
    wide[...] = jnp.zeros_like(wide)
    narrow[...] = jnp.zeros_like(narrow)
    for lev in range(4):
        top = tok[lev, 0:144]
        dn[lev, 0:144] = top
        for side, block in enumerate((tok[lev, 144:288], top)):
            got = nn(pmap[...], block)
            wide[side, lev * 54 : lev * 54 + 54] = got[0:54]
            narrow[side, lev * 18 : lev * 18 + 18] = got[56:74]
        here[lev] = c[lev * 96 : lev * 96 + 48].astype(BF16)
        part = c[lev * 96 + 48 : lev * 96 + 96].astype(BF16)
        dn[lev, 144:192] = part[:, 0:D]
        dn[lev, 192:240] = part[:, D : 2 * D]
    for side in range(2):
        part = c[384 + 24 * side : 408 + 24 * side]
        wide[side, 216:240] = part[:, 0:D]
        wide[side, 240:264] = part[:, D : 2 * D]
    rt[...] = wide[0].astype(BF16)
    dr[...] = wide[1].astype(BF16)
    lf[...] = narrow[0].astype(BF16)
    dl[...] = narrow[1].astype(BF16)


def label(pos, z, bottom):
    row = ((pos % 72 >= 36) & bottom).astype(jnp.int32)
    return row + (2 * (pos // 72).astype(jnp.int32) if z == 1 else 0)


def split_weights(wqkv, w3, wt3):
    eye = (lax.broadcasted_iota(jnp.int32, (D, D), 0) == lax.broadcasted_iota(jnp.int32, (D, D), 1)).astype(BF16)
    for part in range(3):
        w = wqkv[:, part * D : (part + 1) * D]
        w3[part] = w
        wt3[part] = nt(eye, w).astype(BF16)


def prepare_kernel(bottom_ref, wqkv, bias, w3, wt3, bias_t, side_t, low_cols, high_cols):
    split_weights(wqkv, w3, wt3)
    bottom = bottom_ref[0, 0] > 0
    lane = lax.broadcasted_iota(jnp.int32, (1, HQ), 1) % WT
    row = lax.broadcasted_iota(jnp.int32, (WT, 1), 0)
    narrow = lax.broadcasted_iota(jnp.int32, (1, WT), 1) % 24
    narrow = narrow // 12 * 72 + narrow % 12 * 6
    for z in range(2):
        bias_t[z] = jnp.where(label(row, z, bottom) != label(lane, z, bottom), OFF, bias[z].T)
        low_cols[...] = bias[z, :, 0:128]
        high_cols[:, 0 : WT - 128] = bias[z, :, 128:WT]
        for n in range(2):
            every = pl.ds(5 - 5 * n, WT, stride=6)
            table = jnp.concatenate([low_cols[every, :], high_cols[every, :][:, 0 : WT - 128]], axis=1).T
            side_t[n, z] = jnp.where(label(row, z, bottom) != label(narrow, z, bottom), OFF, table)


def staged(kernel, inputs, scalar_count=0):
    def run(*refs):
        scalars, refs = refs[:scalar_count], refs[scalar_count:]
        fetched, rest = refs[:inputs], refs[inputs:]
        places, sems, rest = rest[-inputs - 1 : -1], rest[-1], rest[: -inputs - 1]
        copies = [pltpu.make_async_copy(a, b, sems.at[n]) for n, (a, b) in enumerate(zip(fetched, places))]
        for copy in copies:
            copy.start()

        def arrive(first, last):
            for copy in copies[first:last]:
                copy.wait()

        kernel(arrive, *scalars, *places, *rest)

    return run


def first_kernel(
    arrive, core_ref, own, dn, rt, lf, dr, dl, m_win, gain_one,
    w3, wt3, bias_t, side_t,
    m_head, wproj, m_side, m_sidet, m_sfold, m_pick, m_there,
    m_quad, cot, m_cot, gain_two, wfc1, wfc2t, gain_merge, wmerge, m_back,
    stay, leave, merged, tok8_out, xn_out, prob_out, dout,
    tok8, xn, prob, sent, grads, halo, mixed, tok, side, resq, mlpin, act, dgel, blk, dblk, dpres, dresq, resw, cotq,
):
    arrive(0, 8)

    halo[...] = jnp.zeros_like(halo)
    rt_, lf_, dr_, dl_ = (ref[...].astype(F32) for ref in (rt, lf, dr, dl))
    for lev in range(4):
        z, li = LEVEL_AT[lev]
        halo[0:54] = rt_[lev * 54 : lev * 54 + 54]
        halo[56:74] = lf_[lev * 18 : lev * 18 + 18]
        halo[80:134] = dr_[lev * 54 : lev * 54 + 54]
        halo[136:154] = dl_[lev * 18 : lev * 18 + 18]
        src = jnp.concatenate([own[lev, 144:288], dn[lev, 0:144], halo[...].astype(BF16)], axis=0)
        got = nn(m_win[...], src)
        for win in range(6):
            tok[z * 6 + win, li * 72 : li * 72 + 72] = got[win * 72 : win * 72 + 72]

    g1 = gain_one[...]

    arrive(8, 19)

    def forward(i, carry):
        ws = [i * GROUP + n for n in range(GROUP)]
        zs = [w // 4 for w in ws]
        ts = [tok[z * 6 + w % 4 + 1] for w, z in zip(ws, zs)]
        xs = [(norm_parts(t)[0] * g1).astype(BF16) for t in ts]
        for w, t, x in zip(ws, ts, xs):
            tok8[w] = t.astype(BF16)
            xn[w] = x
        qs = [nn(x, w3[0]).astype(BF16) for x in xs]
        ks = [nn(x, w3[1]).astype(BF16) for x in xs]
        vts = [nt(wt3[2], x).astype(BF16) for x in xs]
        ss = [nt(k, jnp.concatenate([q] * HEADS, axis=0) * m_head[...]) for q, k in zip(qs, ks)]
        ps = []
        for w, z, score in zip(ws, zs, ss):
            e = jnp.exp(score * SCALE + bias_t[z])
            p = (e * (1.0 / jnp.sum(e, axis=0, keepdims=True))).astype(BF16)
            prob[w] = p
            ps.append(p)
        mxs = [by_head(vt, p).astype(BF16) for vt, p in zip(vts, ps)]
        for w, t, mx in zip(ws, ts, mxs):
            mixed[w] = mx
            att = nn(mx, wproj[...]).astype(BF16)
            resw[w] = (t + att.astype(F32)).astype(BF16).astype(F32)
        return carry

    forward(0, 0)
    early = [
        pltpu.make_async_copy(a, b, sent.at[n]) for n, (a, b) in enumerate(((tok8, tok8_out), (xn, xn_out), (prob, prob_out)))
    ]
    for copy in early:
        copy.start()

    beside = [(n, z) for n in range(2) for z in range(2)]
    ts = [tok[z * 6 + 5 * n] for n, z in beside]
    xs = [(norm_parts(t)[0] * g1).astype(BF16) for t in ts]
    qs = [nn(x, w3[0]).astype(BF16) for x in xs]
    ks = [nn(x, w3[1]).astype(BF16) for x in xs]
    vts = [nt(wt3[2], x).astype(BF16) for x in xs]
    ss = [nt(k, nn(m_pick[n], q).astype(BF16) * m_side[...]) for q, k, (n, z) in zip(qs, ks, beside)]
    ps = []
    for score, (n, z) in zip(ss, beside):
        e = jnp.exp(score * SCALE + side_t[n, z])
        ps.append((e * (1.0 / jnp.sum(e, axis=0, keepdims=True))).astype(BF16))
    fulls = [nn(vt, p).astype(BF16) * m_sidet[...] for vt, p in zip(vts, ps)]
    mxs = [nt(m_sfold[...], full).astype(BF16) for full in fulls]
    for t, mx, (n, z) in zip(ts, mxs, beside):
        att = nn(mx, wproj[...]).astype(BF16)
        there = nn(m_there[n], t.astype(BF16))
        side[n, z] = (there + att.astype(F32)).astype(BF16)

    arrive(19, 28)

    for lev in range(4):
        z, li = LEVEL_AT[lev]
        src = jnp.concatenate([resw[z * 4 + win, li * 72 : li * 72 + 72] for win in range(4)], axis=0).astype(BF16)
        src = jnp.concatenate([src, side[0, z, li * 16 : li * 16 + 16], side[1, z, li * 16 : li * 16 + 16]], axis=0)
        got = nn(m_quad[...], src).astype(BF16)
        for k in range(4):
            resq[k, lev * 80 : lev * 80 + 80] = got[k * 80 : k * 80 + 80]

    src = []
    for lev in range(4):
        src += [cot[lev], jnp.concatenate([dn[lev, 144:192], dn[lev, 192:240]], axis=1)]
    for block in (rt_, dr_):
        src.append(jnp.concatenate([block[216:240], block[240:264]], axis=1))
    src = jnp.concatenate(src[:8] + [jnp.concatenate(src[8:], axis=0).astype(BF16)], axis=0)
    cotq[...] = nn(m_cot[...], src).astype(BF16)

    g2 = gain_two[...]
    inner = np.float32(np.sqrt(2 / np.pi))

    def feed(k):
        res = resq[k].astype(F32)
        hat, _ = norm_parts(res)
        mi = (hat * g2).astype(BF16)
        mlpin[k] = mi
        pre = nn(mi, wfc1[...])
        sq = pre * pre
        t = jnp.tanh(pre * (inner + (inner * 0.044715) * sq))
        half = 0.5 + 0.5 * t
        full = pre * half
        a = full.astype(BF16)
        act[k] = a
        dgel[k] = half + full * (1.0 - half) * (2 * inner + (6 * inner * 0.044715) * sq)
        blk[k] = (res + nt(a, wfc2t[...])).astype(BF16)

    for k in range(4):
        feed(k)

    total = 0.0
    for k in range(4):
        total = total + jnp.sum(blk[k].astype(F32), axis=-1, keepdims=True)
    mean = total * (1.0 / 768)
    total = 0.0
    for k in range(4):
        center = blk[k].astype(F32) - mean
        total = total + jnp.sum(center * center, axis=-1, keepdims=True)
    rstd = lax.rsqrt(total * (1.0 / 768) + EPS)
    cq = cotq[...]
    pair = lax.broadcasted_iota(jnp.int32, (320, MG), 0) % 80 % 13
    cq_own = jnp.where(pair < 12, cq.astype(F32), 0.0).astype(BF16)
    out = 0.0
    sum_a = 0.0
    sum_b = 0.0
    hats, gs = [], []
    for k in range(4):
        gm = gain_merge[:, k * D : k * D + D]
        hat = (blk[k].astype(F32) - mean) * rstd
        mn = (hat * gm).astype(BF16)
        wm = wmerge[k * D : k * D + D]
        out = out + nn(mn, wm)
        gmerge = tn(mn, cq_own).astype(BF16)
        for t in range(3):
            at = t * 768 + k * D
            grads[1, at : at + D] = gmerge[:, t * 128 : t * 128 + 128]
        g = nt(cq, wm) * gm
        hats.append(hat)
        gs.append(g)
        sum_a = sum_a + jnp.sum(g, axis=-1, keepdims=True)
        sum_b = sum_b + jnp.sum(g * hat, axis=-1, keepdims=True)
    merged[...] = out.astype(BF16)
    sum_a = sum_a * (1.0 / 768)
    sum_b = sum_b * (1.0 / 768)
    pair = lax.broadcasted_iota(jnp.int32, (320, D), 0) % 80 % 13
    for k in range(4):
        d = rstd * (gs[k] - sum_a - hats[k] * sum_b)
        d = jnp.where(pair == (0 if k % 2 == 0 else 12), 0.0, d)
        db = d.astype(BF16)
        dpre = (nn(db, wfc2t[...]) * dgel[k]).astype(BF16)
        dblk[k] = db
        dpres[k] = dpre
        dmlp = nt(dpre, wfc1[...])
        hat2, rstd2 = norm_parts(resq[k].astype(F32))
        dresq[k] = (db.astype(F32) + norm_back(hat2, rstd2, g2, dmlp)).astype(BF16)
    fc1 = tn(mlpin[...].reshape(1280, D), dpres[...].reshape(1280, FF))
    fc2 = tn(dblk[...].reshape(1280, D), act[...].reshape(1280, FF))
    for base, value in ((0, fc1.astype(BF16)), (1152, fc2.astype(BF16))):
        for t in range(6):
            grads[0, base + t * D : base + t * D + D] = value[:, t * 128 : t * 128 + 128]

    for lev in range(4):
        z, li = LEVEL_AT[lev]
        src = jnp.concatenate([dresq[k, lev * 80 : lev * 80 + 80] for k in range(4)], axis=0)
        got = nn(m_back[...], src)
        for win in range(4):
            resw[z * 4 + win, li * 72 : li * 72 + 72] = got[win * 72 : win * 72 + 72]
    dout[...] = resw[...].astype(BF16)
    grads[:, 2304:HALF] = jnp.zeros((2, HALF - 2304, 128), BF16)
    gproj = tn(mixed[...].reshape(8 * WT, D), dout[...].reshape(8 * WT, D)).astype(BF16)
    grads[0, 2304 : 2304 + D] = gproj[:, 0:128]
    grads[1, 2304 : 2304 + D, 0:64] = gproj[:, 128:192]
    core = core_ref[0, 0]
    stay[...] = grads[core]
    leave[...] = grads[1 - core]
    for copy in early:
        copy.wait()


def second_kernel(
    arrive, w3, wt3, wproj, xn, datt, m_head, prob,
    grads, dqkv,
    gb,
):
    gb[...] = jnp.zeros_like(gb)
    arrive(0, 6)

    def backward(i, carry):
        ws = [i * GROUP + n for n in range(GROUP)]
        xs = [xn[w] for w in ws]
        ups = [datt[w] for w in ws]
        qs = [nn(x, w3[0]).astype(BF16) for x in xs]
        vs = [nn(x, w3[2]).astype(BF16) for x in xs]
        kts = [nt(wt3[1], x).astype(BF16) for x in xs]
        dms = [nt(up, wproj[...]).astype(BF16) for up in ups]
        dmbds = [jnp.concatenate([dm] * HEADS, axis=0) * m_head[...] for dm in dms]
        dps = [nt(v, dmbd) for v, dmbd in zip(vs, dmbds)]
        arrive(6, 7)
        dsbs = []
        for w, dp in zip(ws, dps):
            p = prob[w].astype(F32)
            ds = p * (dp - jnp.sum(dp * p, axis=0, keepdims=True))
            gb[w // 4] += ds
            dsbs.append((ds * SCALE).astype(BF16))
        for w, dmbd in zip(ws, dmbds):
            dqkv[2, w] = nn(prob[w], dmbd).astype(BF16)
        qbds = [jnp.concatenate([q] * HEADS, axis=0) * m_head[...] for q in qs]
        for w, dsb, qbd in zip(ws, dsbs, qbds):
            dqkv[1, w] = nn(dsb, qbd).astype(BF16)
        for w, kt, dsb in zip(ws, kts, dsbs):
            dqkv[0, w] = by_head(kt, dsb).astype(BF16)
        return carry

    backward(0, 0)

    xs = xn[...].reshape(8 * WT, D)
    parts = [tn(xs, dqkv[part].reshape(8 * WT, D)) for part in range(3)]
    value = jnp.concatenate(parts, axis=1).astype(BF16)
    for t in range(4):
        grads[t * D : t * D + D] = value[:, t * 128 : t * 128 + 128]
    grads[768:960, 0:64] = value[:, 512:576]
    grads[768:960, 64:128] = jnp.zeros((D, 64), BF16)
    for z in range(2):
        total = gb[z].astype(BF16)
        for t in range(7):
            tile = total[:, t * 128 : min(t * 128 + 128, HQ)]
            if t == 6:
                tile = jnp.concatenate([tile, jnp.zeros((WT, 896 - HQ), BF16)], axis=1)
            at = BIAS_AT + (z * 7 + t) * WT
            grads[at : at + WT] = tile
    grads[BIAS_AT + 14 * WT :] = jnp.zeros((PEERS * SECOND - BIAS_AT - 14 * WT, 128), BF16)


def third_kernel(
    tok8, datt, dqkv, merged, gain_one, wqkv, m_out, m_merged,
    keep_t, keep_m, to_rt, to_dn, to_dr,
    gt,
):
    g1 = gain_one[...]
    ws = [wqkv[:, part * D : (part + 1) * D] for part in range(3)]
    for w in range(8):
        dnorm = (nt(dqkv[0, w], ws[0]) + nt(dqkv[1, w], ws[1]) + nt(dqkv[2, w], ws[2])).astype(BF16).astype(F32)
        hat, rstd = norm_parts(tok8[w].astype(F32))
        gt[w] = (datt[w].astype(F32) + norm_back(hat, rstd, g1, dnorm)).astype(BF16).astype(F32)

    for lev in range(4):
        z, li = LEVEL_AT[lev]
        src = jnp.concatenate([gt[z * 4 + win, li * 72 : li * 72 + 72] for win in range(4)], axis=0).astype(BF16)
        got = nn(m_out[...], src).astype(BF16)
        keep_t[lev] = got[0:144]
        to_dn[lev, 0:144] = got[144:288]
        to_rt[lev, 0:32] = got[288:320]
        to_dr[lev, 0:32] = got[320:352]
        got = nn(m_merged[...], merged[lev * 80 : lev * 80 + 80]).astype(BF16)
        keep_m[lev] = got[0:48]
        for half in range(2):
            part = got[:, half * D : half * D + D]
            to_dn[lev, 144 + 48 * half : 192 + 48 * half] = part[48:96]
            to_rt[lev, 32 + 16 * half : 48 + 16 * half] = part[96:112]
            to_dr[lev, 32 + 16 * half : 48 + 16 * half] = part[112:128]


def place_kernel(keep_t, keep_m, rt, dn, dr, m_place, m_pm, grad_tokens, merged):
    def halves(ref, lev, start, count):
        return jnp.concatenate([ref[lev, start : start + count], ref[lev, start + count : start + 2 * count]], axis=1)

    for lev in range(4):
        low = keep_t[lev].astype(F32) + nn(m_place[...], rt[lev, 0:32])
        top = dn[lev, 0:144].astype(F32) + nn(m_place[...], dr[lev, 0:32])
        grad_tokens[lev, 0:144] = top.astype(BF16)
        grad_tokens[lev, 144:288] = low.astype(BF16)
    src = [keep_m[lev] for lev in range(4)]
    src += [halves(dn, lev, 144, 48) for lev in range(4)]
    src += [halves(rt, lev, 32, 16) for lev in range(4)]
    src += [halves(dr, lev, 32, 16) for lev in range(4)]
    got = nn(m_pm[...], jnp.concatenate(src, axis=0)).astype(BF16)
    for i in range(72):
        merged[i] = got[4 * i : 4 * i + 4]


def add_kernel(is_weight, got, out, *, bands):
    count = got.shape[0]
    mine = got[0, 0:FIRST].astype(F32)
    for n in range(1, count):
        mine = mine + got[n, 0:FIRST].astype(F32)
    mine = mine.astype(BF16)
    total = 0.0
    parts = []
    for b in range(bands):
        part = got[b, FIRST:ROWS].astype(F32)
        for n in range(b + bands, count, bands):
            part = part + got[n, FIRST:ROWS].astype(F32)
        parts.append(part)
        total = total + part
    flag = is_weight[0, 0] > 0
    for b in range(bands):
        part = jnp.where(flag, total, parts[b]).astype(BF16)
        for n in range(b, count, bands):
            out[n, 0:FIRST] = mine
            out[n, FIRST:ROWS] = part


def pieces(start, count, size):
    while count:
        chunk, off = start // size, start % size
        take = min(count, size - off)
        yield chunk, off, take
        start, count = start + take, count - take


def bias_kernel(buf, gbias, *, scale):
    def rows(start, count):
        got = [buf[c, FIRST + off : FIRST + off + n].astype(F32) for c, off, n in pieces(start, count, SECOND)]
        return jnp.concatenate(got, axis=0)

    for z in range(2):
        for t in range(7):
            part = rows(BIAS_AT + (z * 7 + t) * WT, WT).T * scale
            end = min(t * 128 + 128, HQ)
            gbias[z, t * 128 : end] = part[0 : end - t * 128]


def final_kernel(core_ref, buf, oth, gqkv, gproj, gfc1, gfc2t, gmerge, *, scale):
    here = core_ref[0, 0]

    def first(half, start, count):
        got = []
        for c, off, n in pieces(start, count, FIRST):
            got.append(jnp.where(here == half, buf[c, off : off + n], oth[c, off : off + n]).astype(F32))
        return jnp.concatenate(got, axis=0) * scale

    def second(start, count):
        got = []
        for c, off, n in pieces(start, count, SECOND):
            at = FIRST + off
            got.append(buf[c, at : at + n].astype(F32) + oth[c, at : at + n].astype(F32))
        return jnp.concatenate(got, axis=0) * scale

    for t in range(6):
        gfc1[:, t * 128 : t * 128 + 128] = first(0, t * D, D)
        gfc2t[:, t * 128 : t * 128 + 128] = first(0, 1152 + t * D, D)
    for t in range(3):
        gmerge[:, t * 128 : t * 128 + 128] = first(1, t * 768, 768)
    gproj[:, 0:128] = first(0, 2304, D)
    gproj[:, 128:192] = first(1, 2304, D)[:, 0:64]
    for t in range(5):
        end = min(t * 128 + 128, 576)
        gqkv[:, t * 128 : end] = second(t * D, D)[:, 0 : end - t * 128]


def call(kernel, outs, scratch=(), flops=10**7, size=10**6, limit=16, **more):
    return pl.pallas_call(
        kernel,
        out_shape=outs,
        **more,
        scratch_shapes=list(scratch),
        compiler_params=pltpu.CompilerParams(vmem_limit_bytes=limit * 2**20),
        cost_estimate=pl.CostEstimate(flops=flops, bytes_accessed=size, transcendentals=0),
    )


def shape(*dims, kind=BF16):
    return jax.ShapeDtypeStruct(dims, kind)


def first_call():
    held = pl.BlockSpec(memory_space=pltpu.HBM)
    operands = [
        shape(4, 288, D),
        shape(4, 240, D),
        shape(272, D),
        shape(80, D),
        shape(272, D),
        shape(80, D),
        shape(432, 448),
        shape(1, D, kind=F32),
        shape(3, D, D),
        shape(3, D, D),
        shape(2, WT, HQ, kind=F32),
        shape(2, 2, WT, WT, kind=F32),
        shape(HQ, D),
        shape(D, D),
        shape(WT, D),
        shape(D, WT),
        shape(32, WT),
        shape(2, WT, WT),
        shape(2, 32, WT),
        shape(320, 320),
        shape(4, 48, MG),
        shape(320, 432),
        shape(1, D, kind=F32),
        shape(D, FF),
        shape(D, FF),
        shape(1, FF, kind=F32),
        shape(FF, MG),
        shape(288, 320),
    ]
    count = len(operands)
    return call(
        staged(first_kernel, count, 1),
        (
            shape(HALF, 128),
            shape(HALF, 128),
            shape(320, MG),
            shape(8, WT, D),
            shape(8, WT, D),
            shape(8, WT, HQ),
            shape(8, WT, D),
        ),
        [
            pltpu.VMEM((8, WT, D), BF16),
            pltpu.VMEM((8, WT, D), BF16),
            pltpu.VMEM((8, WT, HQ), BF16),
            pltpu.SemaphoreType.DMA((3,)),
            pltpu.VMEM((2, HALF, 128), BF16),
            pltpu.VMEM((160, D), F32),
            pltpu.VMEM((8, WT, D), BF16),
            pltpu.VMEM((12, WT, D), F32),
            pltpu.VMEM((2, 2, 32, D), BF16),
            pltpu.VMEM((4, 320, D), BF16),
            pltpu.VMEM((4, 320, D), BF16),
            pltpu.VMEM((4, 320, FF), BF16),
            pltpu.VMEM((4, 320, FF), F32),
            pltpu.VMEM((4, 320, D), BF16),
            pltpu.VMEM((4, 320, D), BF16),
            pltpu.VMEM((4, 320, FF), BF16),
            pltpu.VMEM((4, 320, D), BF16),
            pltpu.VMEM((8, WT, D), F32),
            pltpu.VMEM((320, MG), BF16),
        ]
        + [pltpu.VMEM(op.shape, op.dtype) for op in operands]
        + [pltpu.SemaphoreType.DMA((count,))],
        flops=2 * 10**10,
        size=10**7,
        limit=58,
        in_specs=[SCALAR] + [held] * count,
        out_specs=(WHOLE, WHOLE, WHOLE, held, held, held, WHOLE),
    )


def second_call():
    operands = [
        shape(3, D, D),
        shape(3, D, D),
        shape(D, D),
        shape(8, WT, D),
        shape(8, WT, D),
        shape(HQ, D),
        shape(8, WT, HQ),
    ]
    count = len(operands)
    return call(
        staged(second_kernel, count),
        (shape(PEERS * SECOND, 128), shape(3, 8, WT, D)),
        [
            pltpu.VMEM((2, WT, HQ), F32),
        ]
        + [pltpu.VMEM(op.shape, op.dtype) for op in operands]
        + [pltpu.SemaphoreType.DMA((count,))],
        flops=10**10,
        size=10**7,
        limit=58,
        in_specs=[pl.BlockSpec(memory_space=pltpu.HBM)] * count,
    )


def third_call():
    return call(
        third_kernel,
        (shape(4, 144, D), shape(4, 48, MG), shape(4, 64, D), shape(4, 240, D), shape(4, 64, D)),
        [pltpu.VMEM((8, WT, D), F32)],
        flops=10**10,
        size=10**7,
        limit=58,
    )


def body(tokens, gain_one, w_qkv, w_proj, bias_table, gain_two, w_fc1, w_fc2, gain_merge, w_merge, cotangent):
    lat_count = lax.axis_size(LAT)
    lon_count = lax.axis_size("lon")
    count = lat_count * lon_count
    peers = ("lon", "chip")
    bottom = (lax.axis_index(LAT) == lat_count - 1).astype(jnp.int32).reshape(1, 1)
    core = lax.axis_index("core").reshape(1, 1)
    flat = tokens.reshape(4, 288, D)

    def move(block, lon_step, lat_step):
        route = []
        for a in range(lon_count):
            for b in range(lat_count):
                to = (a + lon_step) % lon_count * lat_count + (b + lat_step) % lat_count
                route.append((a * lat_count + b, to))
        return lax.ppermute(block, ("lon",) + LAT, route)

    dn, rt, lf, dr, dl, cot = call(
        pack_kernel,
        (
            shape(4, 240, D),
            shape(272, D),
            shape(80, D),
            shape(272, D),
            shape(80, D),
            shape(4, 48, MG),
        ),
        [pltpu.VMEM((288, MG), F32), pltpu.VMEM((2, 272, D), F32), pltpu.VMEM((2, 80, D), F32)],
        limit=58,
    )(flat, cotangent.transpose(1, 2, 0, 3).reshape(72, 4, MG), pack_map(), pack_cot_map())
    dn = move(dn, 0, -1)
    rt = move(rt, -1, 0)
    lf = move(lf, 1, 0)
    dr = move(dr, -1, -1)
    dl = move(dl, 1, -1)

    head, sidem = head_mask(), side_mask()
    g1 = gain_one.reshape(1, D)
    w3, wt3, bias_t, side_t = call(
        prepare_kernel,
        (shape(3, D, D), shape(3, D, D), shape(2, WT, HQ, kind=F32), shape(2, 2, WT, WT, kind=F32)),
        [pltpu.VMEM((HQ, 128), F32), pltpu.VMEM((HQ, 128), F32)],
        limit=58,
        in_specs=[SCALAR, WHOLE, WHOLE],
    )(bottom, w_qkv, bias_table.reshape(2, HQ, WT))
    first, leave, merged, tok8, xn, prob, datt = first_call()(
        core, flat, dn, rt, lf, dr, dl, window_map(), g1, w3, wt3, bias_t, side_t,
        head, w_proj, sidem, sidem.T, side_fold(),
        jnp.stack([side_pick(5, False), side_pick(0, False)]), jnp.stack([side_pick(5, True), side_pick(0, True)]),
        quad_map(), cot, cot_map(), gain_two.reshape(1, D), w_fc1, w_fc2.T, gain_merge.reshape(1, FF), w_merge, back_map(),
    )
    arrived = lax.ppermute(leave, "core", [(0, 1), (1, 0)])
    second, dqkv = second_call()(w3, wt3, w_proj, xn, datt, head, prob)
    arrived, second = lax.optimization_barrier((arrived, second))
    first = (first.astype(F32) + arrived.astype(F32)).astype(BF16).reshape(PEERS, FIRST, 128)
    grads = jnp.concatenate([first, second.reshape(PEERS, SECOND, 128)], axis=1)
    grads = lax.all_to_all(grads, peers, 0, 0)
    keep_t, keep_m, rt, dn, dr = third_call()(tok8, datt, dqkv, merged, g1, w_qkv, out_map(), merged_map())
    rt = move(rt, 1, 0)
    dn = move(dn, 0, 1)
    dr = move(dr, 1, 1)
    grads, rt, dn, dr = lax.optimization_barrier((grads, rt, dn, dr))
    place = lax.axis_index(peers)
    is_weight = (place < BIAS_AT // SECOND).astype(jnp.int32).reshape(1, 1)
    grads = call(
        functools.partial(add_kernel, bands=lax.axis_size("chip")), shape(PEERS, ROWS, 128), in_specs=[SCALAR, WHOLE]
    )(is_weight, grads)
    grads = lax.all_to_all(grads, peers, 0, 0)
    grad_tokens, merged = call(place_kernel, (shape(4, 288, D), shape(72, 4, MG)))(
        keep_t, keep_m, rt, dn, dr, place_map(), place_merged_map()
    )
    grads, grad_tokens, merged = lax.optimization_barrier((grads, grad_tokens, merged))
    other = lax.ppermute(grads, "core", [(0, 1), (1, 0)])
    gbias = call(
        functools.partial(bias_kernel, scale=WT * (4 * lon_count) ** (-0.5)), shape(2, HQ, WT, kind=F32)
    )(grads)
    gqkv, gproj, gfc1, gfc2t, gmerge = call(
        functools.partial(final_kernel, scale=(1152 * count) ** (-0.5)),
        (
            shape(D, 3 * D, kind=F32),
            shape(D, D, kind=F32),
            shape(D, FF, kind=F32),
            shape(D, FF, kind=F32),
            shape(FF, MG, kind=F32),
        ),
        in_specs=[SCALAR, WHOLE, WHOLE],
    )(core, grads, other)
    return (
        merged.reshape(6, 12, 4, MG).transpose(2, 0, 1, 3),
        grad_tokens.reshape(4, 12, 24, D),
        gqkv,
        gproj,
        gfc1,
        gfc2t.T,
        gmerge,
        gbias.reshape(1, 2, HEADS, WT, WT),
    )


def solution(mesh):
    lons, lats = mesh.devices.shape
    mesh = jax.sharding.Mesh(mesh.devices.reshape(lons, lats // 2, 2), ("lon",) + LAT)
    placed = (
        P(None, LAT, "lon", None),
        P(),
        P(),
        P(),
        P(LAT, None, None, None, None),
        P(),
        P(),
        P(),
        P(),
        P(),
        P(None, LAT, "lon", None),
    )
    return jax.shard_map(
        body,
        mesh=mesh,
        in_specs=placed,
        out_specs=(
            P(None, LAT, "lon", None),
            P(None, LAT, "lon", None),
            P(),
            P(),
            P(),
            P(),
            P(),
            P(LAT, None, None, None, None),
        ),
        check_vma=False,
    )
```

```python
import functools

import jax
import jax.numpy as jnp
import numpy as np
from jax import lax
from jax.experimental import pallas as pl
from jax.experimental.pallas import tpu as pltpu
from jax.sharding import PartitionSpec as P

F32 = jnp.float32
BF16 = jnp.bfloat16
EPS = 1e-05
D = 192
HEADS = 6
HD = 32
WT = 144
HQ = HEADS * WT
FF = 768
MG = 384
SCALE = HD ** (-0.5)
OFF = -1e30
SCALAR = pl.BlockSpec(memory_space=pltpu.SMEM)
WHOLE = pl.BlockSpec(memory_space=pltpu.VMEM)
LAT = ("chip", "core")
GROUP = 8
PEERS = 64
FIRST = 40
SECOND = 48
ROWS = FIRST + SECOND
HALF = PEERS * FIRST
BIAS_AT = 960


def one_hot(shape, pairs):
    table = np.zeros(shape, np.float32)
    for row, col in pairs:
        table[row, col] = 1.0
    return jnp.asarray(table, BF16)


def pack_map():
    pairs = [(r * 9 + c, r * 24 + c) for r in range(6) for c in range(9)]
    pairs += [(56 + r * 3 + c, r * 24 + 21 + c) for r in range(6) for c in range(3)]
    return one_hot((80, 144), pairs)


def pack_cot_map():
    pairs = []
    for lev in range(4):
        for r in range(3):
            for c in range(12):
                pairs.append((lev * 96 + r * 16 + c, ((3 + r) * 12 + c) * 4 + lev))
                pairs.append((lev * 96 + 48 + r * 16 + c, (r * 12 + c) * 4 + lev))
            for c in range(2):
                pairs.append((384 + lev * 6 + r * 2 + c, ((3 + r) * 12 + c) * 4 + lev))
                pairs.append((408 + lev * 6 + r * 2 + c, (r * 12 + c) * 4 + lev))
    return one_hot((432, 288), pairs)


def window_map():
    pairs = []
    for win in range(6):
        for row in range(12):
            for c in range(6):
                e, r = 6 * win + c, row % 6
                upper = row < 6
                if e < 3:
                    src = (344 if upper else 424) + r * 3 + e
                elif e < 27:
                    src = (0 if upper else 144) + r * 24 + e - 3
                else:
                    src = (288 if upper else 368) + r * 9 + e - 27
                pairs.append((win * 72 + row * 6 + c, src))
    return one_hot((432, 448), pairs)


def cot_map():
    pairs = []
    for lev in range(4):
        for r in range(6):
            for p in range(13):
                if p < 11:
                    src = lev * 96 + r * 16 + p + 1
                else:
                    src = (384 if r < 3 else 408) + lev * 6 + r % 3 * 2 + p - 11
                pairs.append((lev * 80 + r * 13 + p, src))
    return one_hot((320, 432), pairs)


def quad_pairs():
    pairs = []
    for ro in range(2):
        for co in range(2):
            for pr in range(6):
                for p in range(13):
                    row, e = 2 * pr + ro, 5 + 2 * p + co
                    if e == 5:
                        src = 288 + row
                    elif e == 30:
                        src = 304 + row
                    else:
                        src = (e - 6) // 6 * 72 + row * 6 + (e - 6) % 6
                    pairs.append(((2 * ro + co) * 80 + pr * 13 + p, src))
    return pairs


def quad_map():
    return one_hot((320, 320), quad_pairs())


def back_map():
    return one_hot((288, 320), [(s, d) for d, s in quad_pairs() if s < 288])


def out_map():
    pairs = []
    for row in range(12):
        for e in range(24):
            src = e // 6 * 72 + row * 6 + e % 6
            r = row % 6
            if e < 21:
                dst = (0 if row < 6 else 144) + r * 24 + e + 3
            else:
                dst = (288 if row < 6 else 320) + r * 3 + e - 21
            pairs.append((dst, src))
    return one_hot((352, 288), pairs)


def merged_map():
    pairs = []
    for r in range(6):
        for p in range(11):
            pairs.append(((0 if r < 3 else 48) + r % 3 * 16 + p + 1, r * 13 + p))
        pairs.append(((96 if r < 3 else 112) + r % 3, r * 13 + 11))
    return one_hot((128, 80), pairs)


def place_map():
    return one_hot((144, 32), [(r * 24 + c, r * 3 + c) for r in range(6) for c in range(3)])


def place_merged_map():
    pairs = []
    for lev in range(4):
        for r in range(6):
            for c in range(12):
                if c:
                    src = (192 if r < 3 else 0) + lev * 48 + r % 3 * 16 + c
                else:
                    src = (448 if r < 3 else 384) + lev * 16 + r % 3
                pairs.append(((r * 12 + c) * 4 + lev, src))
    return one_hot((288, 512), pairs)


def head_mask():
    return one_hot((HQ, D), [(h * WT + q, h * HD + c) for h in range(HEADS) for q in range(WT) for c in range(HD)])


def side_mask():
    return one_hot((WT, D), [(h * 24 + q, h * HD + c) for h in range(HEADS) for q in range(24) for c in range(HD)])


def side_fold():
    pairs = [(li * 16 + r, h * 24 + li * 12 + r) for h in range(HEADS) for li in range(2) for r in range(12)]
    return one_hot((32, WT), pairs)


def side_pick(col, padded):
    step, heads = (16, 1) if padded else (12, HEADS)
    pairs = [
        (h * 2 * step + li * step + r, li * 72 + r * 6 + col)
        for h in range(heads)
        for li in range(2)
        for r in range(12)
    ]
    return one_hot((2 * step * heads, WT), pairs)


def nn(a, b):
    return lax.dot_general(a, b, (((1,), (0,)), ((), ())), preferred_element_type=F32)


def nt(a, b):
    return lax.dot_general(a, b, (((1,), (1,)), ((), ())), preferred_element_type=F32)


def tn(a, b):
    return lax.dot_general(a, b, (((0,), (0,)), ((), ())), preferred_element_type=F32)


def by_head(left, right):
    parts = [nn(left[h * HD : h * HD + HD], right[:, h * WT : h * WT + WT]) for h in range(HEADS)]
    return jnp.concatenate(parts, axis=0).T


def norm_parts(values):
    center = values - jnp.mean(values, axis=-1, keepdims=True)
    rstd = lax.rsqrt(jnp.mean(center * center, axis=-1, keepdims=True) + EPS)
    return center * rstd, rstd


def norm_back(hat, rstd, gain, upstream):
    g = upstream * gain
    return rstd * (g - jnp.mean(g, axis=-1, keepdims=True) - hat * jnp.mean(g * hat, axis=-1, keepdims=True))


LEVEL_AT = ((1, 1), (0, 0), (0, 1), (1, 0))


def pack_kernel(tok, cot, pmap, cmap, dn, rt, lf, dr, dl, here, rows, wide, narrow):
    for i in range(72):
        rows[4 * i : 4 * i + 4] = cot[i].astype(F32)
    c = nn(cmap[...], rows[...].astype(BF16))
    wide[...] = jnp.zeros_like(wide)
    narrow[...] = jnp.zeros_like(narrow)
    for lev in range(4):
        top = tok[lev, 0:144]
        dn[lev, 0:144] = top
        for side, block in enumerate((tok[lev, 144:288], top)):
            got = nn(pmap[...], block)
            wide[side, lev * 54 : lev * 54 + 54] = got[0:54]
            narrow[side, lev * 18 : lev * 18 + 18] = got[56:74]
        here[lev] = c[lev * 96 : lev * 96 + 48].astype(BF16)
        part = c[lev * 96 + 48 : lev * 96 + 96].astype(BF16)
        dn[lev, 144:192] = part[:, 0:D]
        dn[lev, 192:240] = part[:, D : 2 * D]
    for side in range(2):
        part = c[384 + 24 * side : 408 + 24 * side]
        wide[side, 216:240] = part[:, 0:D]
        wide[side, 240:264] = part[:, D : 2 * D]
    rt[...] = wide[0].astype(BF16)
    dr[...] = wide[1].astype(BF16)
    lf[...] = narrow[0].astype(BF16)
    dl[...] = narrow[1].astype(BF16)


def label(pos, z, bottom):
    row = ((pos % 72 >= 36) & bottom).astype(jnp.int32)
    return row + (2 * (pos // 72).astype(jnp.int32) if z == 1 else 0)


def split_weights(wqkv, w3, wt3):
    eye = (lax.broadcasted_iota(jnp.int32, (D, D), 0) == lax.broadcasted_iota(jnp.int32, (D, D), 1)).astype(BF16)
    for part in range(3):
        w = wqkv[:, part * D : (part + 1) * D]
        w3[part] = w
        wt3[part] = nt(eye, w).astype(BF16)


def prepare_kernel(bottom_ref, wqkv, bias, w3, wt3, bias_t, side_t, low_cols, high_cols):
    split_weights(wqkv, w3, wt3)
    bottom = bottom_ref[0, 0] > 0
    lane = lax.broadcasted_iota(jnp.int32, (1, HQ), 1) % WT
    row = lax.broadcasted_iota(jnp.int32, (WT, 1), 0)
    narrow = lax.broadcasted_iota(jnp.int32, (1, WT), 1) % 24
    narrow = narrow // 12 * 72 + narrow % 12 * 6
    for z in range(2):
        bias_t[z] = jnp.where(label(row, z, bottom) != label(lane, z, bottom), OFF, bias[z].T)
        low_cols[...] = bias[z, :, 0:128]
        high_cols[:, 0 : WT - 128] = bias[z, :, 128:WT]
        for n in range(2):
            every = pl.ds(5 - 5 * n, WT, stride=6)
            table = jnp.concatenate([low_cols[every, :], high_cols[every, :][:, 0 : WT - 128]], axis=1).T
            side_t[n, z] = jnp.where(label(row, z, bottom) != label(narrow, z, bottom), OFF, table)


def staged(kernel, inputs, scalar_count=0):
    def run(*refs):
        scalars, refs = refs[:scalar_count], refs[scalar_count:]
        fetched, rest = refs[:inputs], refs[inputs:]
        places, sems, rest = rest[-inputs - 1 : -1], rest[-1], rest[: -inputs - 1]
        copies = [pltpu.make_async_copy(a, b, sems.at[n]) for n, (a, b) in enumerate(zip(fetched, places))]
        for copy in copies:
            copy.start()

        def arrive(first, last):
            for copy in copies[first:last]:
                copy.wait()

        kernel(arrive, *scalars, *places, *rest)

    return run


def first_kernel(
    arrive, core_ref, own, dn, rt, lf, dr, dl, m_win, gain_one,
    w3, wt3, bias_t, side_t,
    m_head, wproj, m_side, m_sidet, m_sfold, m_pick, m_there,
    m_quad, cot, m_cot, gain_two, wfc1, wfc2t, gain_merge, wmerge, m_back,
    stay, leave, merged, tok8_out, xn_out, prob_out, dout,
    tok8, xn, prob, sent, grads, halo, mixed, tok, side, resq, mlpin, act, dgel, blk, dblk, dpres, dresq, resw, cotq,
):
    arrive(0, 8)

    halo[...] = jnp.zeros_like(halo)
    rt_, lf_, dr_, dl_ = (ref[...].astype(F32) for ref in (rt, lf, dr, dl))
    for lev in range(4):
        z, li = LEVEL_AT[lev]
        halo[0:54] = rt_[lev * 54 : lev * 54 + 54]
        halo[56:74] = lf_[lev * 18 : lev * 18 + 18]
        halo[80:134] = dr_[lev * 54 : lev * 54 + 54]
        halo[136:154] = dl_[lev * 18 : lev * 18 + 18]
        src = jnp.concatenate([own[lev, 144:288], dn[lev, 0:144], halo[...].astype(BF16)], axis=0)
        got = nn(m_win[...], src)
        for win in range(6):
            tok[z * 6 + win, li * 72 : li * 72 + 72] = got[win * 72 : win * 72 + 72]

    g1 = gain_one[...]

    arrive(8, 19)

    def forward(i, carry):
        ws = [i * GROUP + n for n in range(GROUP)]
        zs = [w // 4 for w in ws]
        ts = [tok[z * 6 + w % 4 + 1] for w, z in zip(ws, zs)]
        xs = [(norm_parts(t)[0] * g1).astype(BF16) for t in ts]
        for w, t, x in zip(ws, ts, xs):
            tok8[w] = t.astype(BF16)
            xn[w] = x
        qs = [nn(x, w3[0]).astype(BF16) for x in xs]
        ks = [nn(x, w3[1]).astype(BF16) for x in xs]
        vts = [nt(wt3[2], x).astype(BF16) for x in xs]
        ss = [nt(k, jnp.concatenate([q] * HEADS, axis=0) * m_head[...]) for q, k in zip(qs, ks)]
        ps = []
        for w, z, score in zip(ws, zs, ss):
            e = jnp.exp(score * SCALE + bias_t[z])
            p = (e * (1.0 / jnp.sum(e, axis=0, keepdims=True))).astype(BF16)
            prob[w] = p
            ps.append(p)
        mxs = [by_head(vt, p).astype(BF16) for vt, p in zip(vts, ps)]
        for w, t, mx in zip(ws, ts, mxs):
            mixed[w] = mx
            att = nn(mx, wproj[...]).astype(BF16)
            resw[w] = (t + att.astype(F32)).astype(BF16).astype(F32)
        return carry

    forward(0, 0)
    early = [
        pltpu.make_async_copy(a, b, sent.at[n]) for n, (a, b) in enumerate(((tok8, tok8_out), (xn, xn_out), (prob, prob_out)))
    ]
    for copy in early:
        copy.start()

    beside = [(n, z) for n in range(2) for z in range(2)]
    ts = [tok[z * 6 + 5 * n] for n, z in beside]
    xs = [(norm_parts(t)[0] * g1).astype(BF16) for t in ts]
    qs = [nn(x, w3[0]).astype(BF16) for x in xs]
    ks = [nn(x, w3[1]).astype(BF16) for x in xs]
    vts = [nt(wt3[2], x).astype(BF16) for x in xs]
    ss = [nt(k, nn(m_pick[n], q).astype(BF16) * m_side[...]) for q, k, (n, z) in zip(qs, ks, beside)]
    ps = []
    for score, (n, z) in zip(ss, beside):
        e = jnp.exp(score * SCALE + side_t[n, z])
        ps.append((e * (1.0 / jnp.sum(e, axis=0, keepdims=True))).astype(BF16))
    fulls = [nn(vt, p).astype(BF16) * m_sidet[...] for vt, p in zip(vts, ps)]
    mxs = [nt(m_sfold[...], full).astype(BF16) for full in fulls]
    for t, mx, (n, z) in zip(ts, mxs, beside):
        att = nn(mx, wproj[...]).astype(BF16)
        there = nn(m_there[n], t.astype(BF16))
        side[n, z] = (there + att.astype(F32)).astype(BF16)

    arrive(19, 28)

    for lev in range(4):
        z, li = LEVEL_AT[lev]
        src = jnp.concatenate([resw[z * 4 + win, li * 72 : li * 72 + 72] for win in range(4)], axis=0).astype(BF16)
        src = jnp.concatenate([src, side[0, z, li * 16 : li * 16 + 16], side[1, z, li * 16 : li * 16 + 16]], axis=0)
        got = nn(m_quad[...], src).astype(BF16)
        for k in range(4):
            resq[k, lev * 80 : lev * 80 + 80] = got[k * 80 : k * 80 + 80]

    src = []
    for lev in range(4):
        src += [cot[lev], jnp.concatenate([dn[lev, 144:192], dn[lev, 192:240]], axis=1)]
    for block in (rt_, dr_):
        src.append(jnp.concatenate([block[216:240], block[240:264]], axis=1))
    src = jnp.concatenate(src[:8] + [jnp.concatenate(src[8:], axis=0).astype(BF16)], axis=0)
    cotq[...] = nn(m_cot[...], src).astype(BF16)

    g2 = gain_two[...]
    inner = np.float32(np.sqrt(2 / np.pi))

    def feed(k):
        res = resq[k].astype(F32)
        hat, _ = norm_parts(res)
        mi = (hat * g2).astype(BF16)
        mlpin[k] = mi
        pre = nn(mi, wfc1[...])
        sq = pre * pre
        t = jnp.tanh(pre * (inner + (inner * 0.044715) * sq))
        half = 0.5 + 0.5 * t
        full = pre * half
        a = full.astype(BF16)
        act[k] = a
        dgel[k] = half + full * (1.0 - half) * (2 * inner + (6 * inner * 0.044715) * sq)
        blk[k] = (res + nt(a, wfc2t[...])).astype(BF16)

    for k in range(4):
        feed(k)

    total = 0.0
    for k in range(4):
        total = total + jnp.sum(blk[k].astype(F32), axis=-1, keepdims=True)
    mean = total * (1.0 / 768)
    total = 0.0
    for k in range(4):
        center = blk[k].astype(F32) - mean
        total = total + jnp.sum(center * center, axis=-1, keepdims=True)
    rstd = lax.rsqrt(total * (1.0 / 768) + EPS)
    cq = cotq[...]
    pair = lax.broadcasted_iota(jnp.int32, (320, MG), 0) % 80 % 13
    cq_own = jnp.where(pair < 12, cq.astype(F32), 0.0).astype(BF16)
    out = 0.0
    sum_a = 0.0
    sum_b = 0.0
    hats, gs = [], []
    for k in range(4):
        gm = gain_merge[:, k * D : k * D + D]
        hat = (blk[k].astype(F32) - mean) * rstd
        mn = (hat * gm).astype(BF16)
        wm = wmerge[k * D : k * D + D]
        out = out + nn(mn, wm)
        gmerge = tn(mn, cq_own).astype(BF16)
        for t in range(3):
            at = t * 768 + k * D
            grads[1, at : at + D] = gmerge[:, t * 128 : t * 128 + 128]
        g = nt(cq, wm) * gm
        hats.append(hat)
        gs.append(g)
        sum_a = sum_a + jnp.sum(g, axis=-1, keepdims=True)
        sum_b = sum_b + jnp.sum(g * hat, axis=-1, keepdims=True)
    merged[...] = out.astype(BF16)
    sum_a = sum_a * (1.0 / 768)
    sum_b = sum_b * (1.0 / 768)
    pair = lax.broadcasted_iota(jnp.int32, (320, D), 0) % 80 % 13
    for k in range(4):
        d = rstd * (gs[k] - sum_a - hats[k] * sum_b)
        d = jnp.where(pair == (0 if k % 2 == 0 else 12), 0.0, d)
        db = d.astype(BF16)
        dpre = (nn(db, wfc2t[...]) * dgel[k]).astype(BF16)
        dblk[k] = db
        dpres[k] = dpre
        dmlp = nt(dpre, wfc1[...])
        hat2, rstd2 = norm_parts(resq[k].astype(F32))
        dresq[k] = (db.astype(F32) + norm_back(hat2, rstd2, g2, dmlp)).astype(BF16)
    fc1 = tn(mlpin[...].reshape(1280, D), dpres[...].reshape(1280, FF))
    fc2 = tn(dblk[...].reshape(1280, D), act[...].reshape(1280, FF))
    for base, value in ((0, fc1.astype(BF16)), (1152, fc2.astype(BF16))):
        for t in range(6):
            grads[0, base + t * D : base + t * D + D] = value[:, t * 128 : t * 128 + 128]

    for lev in range(4):
        z, li = LEVEL_AT[lev]
        src = jnp.concatenate([dresq[k, lev * 80 : lev * 80 + 80] for k in range(4)], axis=0)
        got = nn(m_back[...], src)
        for win in range(4):
            resw[z * 4 + win, li * 72 : li * 72 + 72] = got[win * 72 : win * 72 + 72]
    dout[...] = resw[...].astype(BF16)
    grads[:, 2304:HALF] = jnp.zeros((2, HALF - 2304, 128), BF16)
    gproj = tn(mixed[...].reshape(8 * WT, D), dout[...].reshape(8 * WT, D)).astype(BF16)
    grads[0, 2304 : 2304 + D] = gproj[:, 0:128]
    grads[1, 2304 : 2304 + D, 0:64] = gproj[:, 128:192]
    core = core_ref[0, 0]
    stay[...] = grads[core]
    leave[...] = grads[1 - core]
    for copy in early:
        copy.wait()


def second_kernel(
    arrive, w3, wt3, wproj, xn, datt, m_head, prob,
    grads, dqkv,
    gb,
):
    gb[...] = jnp.zeros_like(gb)
    arrive(0, 6)

    def backward(i, carry):
        ws = [i * GROUP + n for n in range(GROUP)]
        xs = [xn[w] for w in ws]
        ups = [datt[w] for w in ws]
        qs = [nn(x, w3[0]).astype(BF16) for x in xs]
        vs = [nn(x, w3[2]).astype(BF16) for x in xs]
        kts = [nt(wt3[1], x).astype(BF16) for x in xs]
        dms = [nt(up, wproj[...]).astype(BF16) for up in ups]
        dmbds = [jnp.concatenate([dm] * HEADS, axis=0) * m_head[...] for dm in dms]
        dps = [nt(v, dmbd) for v, dmbd in zip(vs, dmbds)]
        arrive(6, 7)
        dsbs = []
        for w, dp in zip(ws, dps):
            p = prob[w].astype(F32)
            ds = p * (dp - jnp.sum(dp * p, axis=0, keepdims=True))
            gb[w // 4] += ds
            dsbs.append((ds * SCALE).astype(BF16))
        for w, dmbd in zip(ws, dmbds):
            dqkv[2, w] = nn(prob[w], dmbd).astype(BF16)
        qbds = [jnp.concatenate([q] * HEADS, axis=0) * m_head[...] for q in qs]
        for w, dsb, qbd in zip(ws, dsbs, qbds):
            dqkv[1, w] = nn(dsb, qbd).astype(BF16)
        for w, kt, dsb in zip(ws, kts, dsbs):
            dqkv[0, w] = by_head(kt, dsb).astype(BF16)
        return carry

    backward(0, 0)

    xs = xn[...].reshape(8 * WT, D)
    parts = [tn(xs, dqkv[part].reshape(8 * WT, D)) for part in range(3)]
    value = jnp.concatenate(parts, axis=1).astype(BF16)
    def put(start, block):
        for n in range(block.shape[0] // SECOND):
            grads[start // SECOND + n, 0:SECOND] = block[n * SECOND : n * SECOND + SECOND]

    for t in range(4):
        put(t * D, value[:, t * 128 : t * 128 + 128])
    put(768, jnp.concatenate([value[:, 512:576], jnp.zeros((D, 64), BF16)], axis=1))
    for z in range(2):
        total = gb[z].astype(BF16)
        for t in range(7):
            tile = total[:, t * 128 : min(t * 128 + 128, HQ)]
            if t == 6:
                tile = jnp.concatenate([tile, jnp.zeros((WT, 896 - HQ), BF16)], axis=1)
            put(BIAS_AT + (z * 7 + t) * WT, tile)
    end = BIAS_AT + 14 * WT
    put(end, jnp.zeros((PEERS * SECOND - end, 128), BF16))


def third_kernel(
    tok8, datt, dqkv, merged, gain_one, wqkv, m_out, m_merged,
    keep_t, keep_m, to_rt, to_dn, to_dr,
    gt,
):
    g1 = gain_one[...]
    ws = [wqkv[:, part * D : (part + 1) * D] for part in range(3)]
    for w in range(8):
        dnorm = (nt(dqkv[0, w], ws[0]) + nt(dqkv[1, w], ws[1]) + nt(dqkv[2, w], ws[2])).astype(BF16).astype(F32)
        hat, rstd = norm_parts(tok8[w].astype(F32))
        gt[w] = (datt[w].astype(F32) + norm_back(hat, rstd, g1, dnorm)).astype(BF16).astype(F32)

    for lev in range(4):
        z, li = LEVEL_AT[lev]
        src = jnp.concatenate([gt[z * 4 + win, li * 72 : li * 72 + 72] for win in range(4)], axis=0).astype(BF16)
        got = nn(m_out[...], src).astype(BF16)
        keep_t[lev] = got[0:144]
        to_dn[lev, 0:144] = got[144:288]
        to_rt[lev, 0:32] = got[288:320]
        to_dr[lev, 0:32] = got[320:352]
        got = nn(m_merged[...], merged[lev * 80 : lev * 80 + 80]).astype(BF16)
        keep_m[lev] = got[0:48]
        for half in range(2):
            part = got[:, half * D : half * D + D]
            to_dn[lev, 144 + 48 * half : 192 + 48 * half] = part[48:96]
            to_rt[lev, 32 + 16 * half : 48 + 16 * half] = part[96:112]
            to_dr[lev, 32 + 16 * half : 48 + 16 * half] = part[112:128]


def place_kernel(keep_t, keep_m, rt, dn, dr, m_place, m_pm, grad_tokens, merged):
    def halves(ref, lev, start, count):
        return jnp.concatenate([ref[lev, start : start + count], ref[lev, start + count : start + 2 * count]], axis=1)

    for lev in range(4):
        low = keep_t[lev].astype(F32) + nn(m_place[...], rt[lev, 0:32])
        top = dn[lev, 0:144].astype(F32) + nn(m_place[...], dr[lev, 0:32])
        grad_tokens[lev, 0:144] = top.astype(BF16)
        grad_tokens[lev, 144:288] = low.astype(BF16)
    src = [keep_m[lev] for lev in range(4)]
    src += [halves(dn, lev, 144, 48) for lev in range(4)]
    src += [halves(rt, lev, 32, 16) for lev in range(4)]
    src += [halves(dr, lev, 32, 16) for lev in range(4)]
    got = nn(m_pm[...], jnp.concatenate(src, axis=0)).astype(BF16)
    for i in range(72):
        merged[i] = got[4 * i : 4 * i + 4]


def add_kernel(is_weight, got, out, *, bands):
    count = got.shape[0]
    mine = got[0, SECOND:ROWS].astype(F32)
    for n in range(1, count):
        mine = mine + got[n, SECOND:ROWS].astype(F32)
    mine = mine.astype(BF16)
    total = 0.0
    parts = []
    for b in range(bands):
        part = got[b, 0:SECOND].astype(F32)
        for n in range(b + bands, count, bands):
            part = part + got[n, 0:SECOND].astype(F32)
        parts.append(part)
        total = total + part
    flag = is_weight[0, 0] > 0
    for b in range(bands):
        part = jnp.where(flag, total, parts[b]).astype(BF16)
        for n in range(b, count, bands):
            out[n, SECOND:ROWS] = mine
            out[n, 0:SECOND] = part


def pieces(start, count, size):
    while count:
        chunk, off = start // size, start % size
        take = min(count, size - off)
        yield chunk, off, take
        start, count = start + take, count - take


def bias_kernel(buf, gbias, *, scale):
    def rows(start, count):
        got = [buf[c, off : off + n].astype(F32) for c, off, n in pieces(start, count, SECOND)]
        return jnp.concatenate(got, axis=0)

    for z in range(2):
        for t in range(7):
            part = rows(BIAS_AT + (z * 7 + t) * WT, WT).T * scale
            end = min(t * 128 + 128, HQ)
            gbias[z, t * 128 : end] = part[0 : end - t * 128]


def final_kernel(core_ref, buf, oth, gqkv, gproj, gfc1, gfc2t, gmerge, *, scale):
    here = core_ref[0, 0]

    def first(half, start, count):
        got = []
        for c, off, n in pieces(start, count, FIRST):
            at = SECOND + off
            got.append(jnp.where(here == half, buf[c, at : at + n], oth[c, at : at + n]).astype(F32))
        return jnp.concatenate(got, axis=0) * scale

    def second(start, count):
        got = []
        for c, off, n in pieces(start, count, SECOND):
            got.append(buf[c, off : off + n].astype(F32) + oth[c, off : off + n].astype(F32))
        return jnp.concatenate(got, axis=0) * scale

    for t in range(6):
        gfc1[:, t * 128 : t * 128 + 128] = first(0, t * D, D)
        gfc2t[:, t * 128 : t * 128 + 128] = first(0, 1152 + t * D, D)
    for t in range(3):
        gmerge[:, t * 128 : t * 128 + 128] = first(1, t * 768, 768)
    gproj[:, 0:128] = first(0, 2304, D)
    gproj[:, 128:192] = first(1, 2304, D)[:, 0:64]
    for t in range(5):
        end = min(t * 128 + 128, 576)
        gqkv[:, t * 128 : end] = second(t * D, D)[:, 0 : end - t * 128]


def call(kernel, outs, scratch=(), flops=10**7, size=10**6, limit=16, **more):
    return pl.pallas_call(
        kernel,
        out_shape=outs,
        **more,
        scratch_shapes=list(scratch),
        compiler_params=pltpu.CompilerParams(vmem_limit_bytes=limit * 2**20),
        cost_estimate=pl.CostEstimate(flops=flops, bytes_accessed=size, transcendentals=0),
    )


def shape(*dims, kind=BF16):
    return jax.ShapeDtypeStruct(dims, kind)


def first_call():
    held = pl.BlockSpec(memory_space=pltpu.HBM)
    operands = [
        shape(4, 288, D),
        shape(4, 240, D),
        shape(272, D),
        shape(80, D),
        shape(272, D),
        shape(80, D),
        shape(432, 448),
        shape(1, D, kind=F32),
        shape(3, D, D),
        shape(3, D, D),
        shape(2, WT, HQ, kind=F32),
        shape(2, 2, WT, WT, kind=F32),
        shape(HQ, D),
        shape(D, D),
        shape(WT, D),
        shape(D, WT),
        shape(32, WT),
        shape(2, WT, WT),
        shape(2, 32, WT),
        shape(320, 320),
        shape(4, 48, MG),
        shape(320, 432),
        shape(1, D, kind=F32),
        shape(D, FF),
        shape(D, FF),
        shape(1, FF, kind=F32),
        shape(FF, MG),
        shape(288, 320),
    ]
    count = len(operands)
    return call(
        staged(first_kernel, count, 1),
        (
            shape(HALF, 128),
            shape(HALF, 128),
            shape(320, MG),
            shape(8, WT, D),
            shape(8, WT, D),
            shape(8, WT, HQ),
            shape(8, WT, D),
        ),
        [
            pltpu.VMEM((8, WT, D), BF16),
            pltpu.VMEM((8, WT, D), BF16),
            pltpu.VMEM((8, WT, HQ), BF16),
            pltpu.SemaphoreType.DMA((3,)),
            pltpu.VMEM((2, HALF, 128), BF16),
            pltpu.VMEM((160, D), F32),
            pltpu.VMEM((8, WT, D), BF16),
            pltpu.VMEM((12, WT, D), F32),
            pltpu.VMEM((2, 2, 32, D), BF16),
            pltpu.VMEM((4, 320, D), BF16),
            pltpu.VMEM((4, 320, D), BF16),
            pltpu.VMEM((4, 320, FF), BF16),
            pltpu.VMEM((4, 320, FF), F32),
            pltpu.VMEM((4, 320, D), BF16),
            pltpu.VMEM((4, 320, D), BF16),
            pltpu.VMEM((4, 320, FF), BF16),
            pltpu.VMEM((4, 320, D), BF16),
            pltpu.VMEM((8, WT, D), F32),
            pltpu.VMEM((320, MG), BF16),
        ]
        + [pltpu.VMEM(op.shape, op.dtype) for op in operands]
        + [pltpu.SemaphoreType.DMA((count,))],
        flops=2 * 10**10,
        size=10**7,
        limit=58,
        in_specs=[SCALAR] + [held] * count,
        out_specs=(WHOLE, WHOLE, WHOLE, held, held, held, WHOLE),
    )


def second_call():
    operands = [
        shape(3, D, D),
        shape(3, D, D),
        shape(D, D),
        shape(8, WT, D),
        shape(8, WT, D),
        shape(HQ, D),
        shape(8, WT, HQ),
    ]
    count = len(operands)
    return call(
        staged(second_kernel, count),
        (shape(PEERS, ROWS, 128), shape(3, 8, WT, D)),
        [
            pltpu.VMEM((2, WT, HQ), F32),
        ]
        + [pltpu.VMEM(op.shape, op.dtype) for op in operands]
        + [pltpu.SemaphoreType.DMA((count,))],
        flops=10**10,
        size=10**7,
        limit=58,
        in_specs=[pl.BlockSpec(memory_space=pltpu.HBM)] * count,
    )


def third_call():
    return call(
        third_kernel,
        (shape(4, 144, D), shape(4, 48, MG), shape(4, 64, D), shape(4, 240, D), shape(4, 64, D)),
        [pltpu.VMEM((8, WT, D), F32)],
        flops=10**10,
        size=10**7,
        limit=58,
    )


def body(tokens, gain_one, w_qkv, w_proj, bias_table, gain_two, w_fc1, w_fc2, gain_merge, w_merge, cotangent):
    lat_count = lax.axis_size(LAT)
    lon_count = lax.axis_size("lon")
    count = lat_count * lon_count
    peers = ("lon", "chip")
    bottom = (lax.axis_index(LAT) == lat_count - 1).astype(jnp.int32).reshape(1, 1)
    core = lax.axis_index("core").reshape(1, 1)
    flat = tokens.reshape(4, 288, D)

    def move(block, lon_step, lat_step):
        route = []
        for a in range(lon_count):
            for b in range(lat_count):
                to = (a + lon_step) % lon_count * lat_count + (b + lat_step) % lat_count
                route.append((a * lat_count + b, to))
        return lax.ppermute(block, ("lon",) + LAT, route)

    dn, rt, lf, dr, dl, cot = call(
        pack_kernel,
        (
            shape(4, 240, D),
            shape(272, D),
            shape(80, D),
            shape(272, D),
            shape(80, D),
            shape(4, 48, MG),
        ),
        [pltpu.VMEM((288, MG), F32), pltpu.VMEM((2, 272, D), F32), pltpu.VMEM((2, 80, D), F32)],
        limit=58,
    )(flat, cotangent.transpose(1, 2, 0, 3).reshape(72, 4, MG), pack_map(), pack_cot_map())
    dn = move(dn, 0, -1)
    rt = move(rt, -1, 0)
    lf = move(lf, 1, 0)
    dr = move(dr, -1, -1)
    dl = move(dl, 1, -1)

    head, sidem = head_mask(), side_mask()
    g1 = gain_one.reshape(1, D)
    w3, wt3, bias_t, side_t = call(
        prepare_kernel,
        (shape(3, D, D), shape(3, D, D), shape(2, WT, HQ, kind=F32), shape(2, 2, WT, WT, kind=F32)),
        [pltpu.VMEM((HQ, 128), F32), pltpu.VMEM((HQ, 128), F32)],
        limit=58,
        in_specs=[SCALAR, WHOLE, WHOLE],
    )(bottom, w_qkv, bias_table.reshape(2, HQ, WT))
    first, leave, merged, tok8, xn, prob, datt = first_call()(
        core, flat, dn, rt, lf, dr, dl, window_map(), g1, w3, wt3, bias_t, side_t,
        head, w_proj, sidem, sidem.T, side_fold(),
        jnp.stack([side_pick(5, False), side_pick(0, False)]), jnp.stack([side_pick(5, True), side_pick(0, True)]),
        quad_map(), cot, cot_map(), gain_two.reshape(1, D), w_fc1, w_fc2.T, gain_merge.reshape(1, FF), w_merge, back_map(),
    )
    arrived = lax.ppermute(leave, "core", [(0, 1), (1, 0)])
    grads, dqkv = second_call()(w3, wt3, w_proj, xn, datt, head, prob)
    arrived, grads = lax.optimization_barrier((arrived, grads))
    first = (first.astype(F32) + arrived.astype(F32)).astype(BF16).reshape(PEERS, FIRST, 128)
    grads = lax.dynamic_update_slice(grads, first, (0, SECOND, 0))
    grads = lax.all_to_all(grads, peers, 0, 0)
    keep_t, keep_m, rt, dn, dr = third_call()(tok8, datt, dqkv, merged, g1, w_qkv, out_map(), merged_map())
    rt = move(rt, 1, 0)
    dn = move(dn, 0, 1)
    dr = move(dr, 1, 1)
    grads, keep_t = lax.optimization_barrier((grads, keep_t))
    place = lax.axis_index(peers)
    is_weight = (place < BIAS_AT // SECOND).astype(jnp.int32).reshape(1, 1)
    grads = call(
        functools.partial(add_kernel, bands=lax.axis_size("chip")), shape(PEERS, ROWS, 128), in_specs=[SCALAR, WHOLE]
    )(is_weight, grads)
    grads = lax.all_to_all(grads, peers, 0, 0)
    grad_tokens, merged = call(place_kernel, (shape(4, 288, D), shape(72, 4, MG)))(
        keep_t, keep_m, rt, dn, dr, place_map(), place_merged_map()
    )
    grads, grad_tokens, merged = lax.optimization_barrier((grads, grad_tokens, merged))
    other = lax.ppermute(grads, "core", [(0, 1), (1, 0)])
    gbias = call(
        functools.partial(bias_kernel, scale=WT * (4 * lon_count) ** (-0.5)), shape(2, HQ, WT, kind=F32)
    )(grads)
    gqkv, gproj, gfc1, gfc2t, gmerge = call(
        functools.partial(final_kernel, scale=(1152 * count) ** (-0.5)),
        (
            shape(D, 3 * D, kind=F32),
            shape(D, D, kind=F32),
            shape(D, FF, kind=F32),
            shape(D, FF, kind=F32),
            shape(FF, MG, kind=F32),
        ),
        in_specs=[SCALAR, WHOLE, WHOLE],
    )(core, grads, other)
    return (
        merged.reshape(6, 12, 4, MG).transpose(2, 0, 1, 3),
        grad_tokens.reshape(4, 12, 24, D),
        gqkv,
        gproj,
        gfc1,
        gfc2t.T,
        gmerge,
        gbias.reshape(1, 2, HEADS, WT, WT),
    )


def solution(mesh):
    lons, lats = mesh.devices.shape
    mesh = jax.sharding.Mesh(mesh.devices.reshape(lons, lats // 2, 2), ("lon",) + LAT)
    placed = (
        P(None, LAT, "lon", None),
        P(),
        P(),
        P(),
        P(LAT, None, None, None, None),
        P(),
        P(),
        P(),
        P(),
        P(),
        P(None, LAT, "lon", None),
    )
    return jax.shard_map(
        body,
        mesh=mesh,
        in_specs=placed,
        out_specs=(
            P(None, LAT, "lon", None),
            P(None, LAT, "lon", None),
            P(),
            P(),
            P(),
            P(),
            P(),
            P(LAT, None, None, None, None),
        ),
        check_vma=False,
    )
```

```python
import functools

import jax
import jax.numpy as jnp
import numpy as np
from jax import lax
from jax.experimental import pallas as pl
from jax.experimental.pallas import tpu as pltpu
from jax.sharding import PartitionSpec as P

F32 = jnp.float32
BF16 = jnp.bfloat16
EPS = 1e-05
D = 192
HEADS = 6
HD = 32
WT = 144
HQ = HEADS * WT
FF = 768
MG = 384
SCALE = HD ** (-0.5)
OFF = -1e30
SCALAR = pl.BlockSpec(memory_space=pltpu.SMEM)
WHOLE = pl.BlockSpec(memory_space=pltpu.VMEM)
LAT = ("chip", "core")
GROUP = 8
PEERS = 64
FIRST = 40
SECOND = 48
ROWS = FIRST + SECOND
HALF = PEERS * FIRST
BIAS_AT = 960


def one_hot(shape, pairs):
    table = np.zeros(shape, np.float32)
    for row, col in pairs:
        table[row, col] = 1.0
    return jnp.asarray(table, BF16)


def pack_map():
    pairs = [(r * 9 + c, r * 24 + c) for r in range(6) for c in range(9)]
    pairs += [(56 + r * 3 + c, r * 24 + 21 + c) for r in range(6) for c in range(3)]
    return one_hot((80, 144), pairs)


def pack_cot_map():
    pairs = []
    for lev in range(4):
        for r in range(3):
            for c in range(12):
                pairs.append((lev * 96 + r * 16 + c, ((3 + r) * 12 + c) * 4 + lev))
                pairs.append((lev * 96 + 48 + r * 16 + c, (r * 12 + c) * 4 + lev))
            for c in range(2):
                pairs.append((384 + lev * 6 + r * 2 + c, ((3 + r) * 12 + c) * 4 + lev))
                pairs.append((408 + lev * 6 + r * 2 + c, (r * 12 + c) * 4 + lev))
    return one_hot((432, 288), pairs)


def window_map():
    pairs = []
    for win in range(6):
        for row in range(12):
            for c in range(6):
                e, r = 6 * win + c, row % 6
                upper = row < 6
                if e < 3:
                    src = (344 if upper else 424) + r * 3 + e
                elif e < 27:
                    src = (0 if upper else 144) + r * 24 + e - 3
                else:
                    src = (288 if upper else 368) + r * 9 + e - 27
                pairs.append((win * 72 + row * 6 + c, src))
    return one_hot((432, 448), pairs)


def cot_map():
    pairs = []
    for lev in range(4):
        for r in range(6):
            for p in range(13):
                if p < 11:
                    src = lev * 96 + r * 16 + p + 1
                else:
                    src = (384 if r < 3 else 408) + lev * 6 + r % 3 * 2 + p - 11
                pairs.append((lev * 80 + r * 13 + p, src))
    return one_hot((320, 432), pairs)


def quad_pairs():
    pairs = []
    for ro in range(2):
        for co in range(2):
            for pr in range(6):
                for p in range(13):
                    row, e = 2 * pr + ro, 5 + 2 * p + co
                    if e == 5:
                        src = 288 + row
                    elif e == 30:
                        src = 304 + row
                    else:
                        src = (e - 6) // 6 * 72 + row * 6 + (e - 6) % 6
                    pairs.append(((2 * ro + co) * 80 + pr * 13 + p, src))
    return pairs


def quad_map():
    return one_hot((320, 320), quad_pairs())


def back_map():
    return one_hot((288, 320), [(s, d) for d, s in quad_pairs() if s < 288])


def out_map():
    pairs = []
    for row in range(12):
        for e in range(24):
            src = e // 6 * 72 + row * 6 + e % 6
            r = row % 6
            if e < 21:
                dst = (0 if row < 6 else 144) + r * 24 + e + 3
            else:
                dst = (288 if row < 6 else 320) + r * 3 + e - 21
            pairs.append((dst, src))
    return one_hot((352, 288), pairs)


def merged_map():
    pairs = []
    for r in range(6):
        for p in range(11):
            pairs.append(((0 if r < 3 else 48) + r % 3 * 16 + p + 1, r * 13 + p))
        pairs.append(((96 if r < 3 else 112) + r % 3, r * 13 + 11))
    return one_hot((128, 80), pairs)


def place_map():
    return one_hot((144, 32), [(r * 24 + c, r * 3 + c) for r in range(6) for c in range(3)])


def place_merged_map():
    pairs = []
    for lev in range(4):
        for r in range(6):
            for c in range(12):
                if c:
                    src = (192 if r < 3 else 0) + lev * 48 + r % 3 * 16 + c
                else:
                    src = (448 if r < 3 else 384) + lev * 16 + r % 3
                pairs.append(((r * 12 + c) * 4 + lev, src))
    return one_hot((288, 512), pairs)


def head_mask():
    return one_hot((HQ, D), [(h * WT + q, h * HD + c) for h in range(HEADS) for q in range(WT) for c in range(HD)])


def side_mask():
    return one_hot((WT, D), [(h * 24 + q, h * HD + c) for h in range(HEADS) for q in range(24) for c in range(HD)])


def side_fold():
    pairs = [(li * 16 + r, h * 24 + li * 12 + r) for h in range(HEADS) for li in range(2) for r in range(12)]
    return one_hot((32, WT), pairs)


def side_pick(col, padded):
    step, heads = (16, 1) if padded else (12, HEADS)
    pairs = [
        (h * 2 * step + li * step + r, li * 72 + r * 6 + col)
        for h in range(heads)
        for li in range(2)
        for r in range(12)
    ]
    return one_hot((2 * step * heads, WT), pairs)


def nn(a, b):
    return lax.dot_general(a, b, (((1,), (0,)), ((), ())), preferred_element_type=F32)


def nt(a, b):
    return lax.dot_general(a, b, (((1,), (1,)), ((), ())), preferred_element_type=F32)


def tn(a, b):
    return lax.dot_general(a, b, (((0,), (0,)), ((), ())), preferred_element_type=F32)


def by_head(left, right):
    parts = [nn(left[h * HD : h * HD + HD], right[:, h * WT : h * WT + WT]) for h in range(HEADS)]
    return jnp.concatenate(parts, axis=0).T


def norm_parts(values):
    center = values - jnp.mean(values, axis=-1, keepdims=True)
    rstd = lax.rsqrt(jnp.mean(center * center, axis=-1, keepdims=True) + EPS)
    return center * rstd, rstd


def norm_back(hat, rstd, gain, upstream):
    g = upstream * gain
    return rstd * (g - jnp.mean(g, axis=-1, keepdims=True) - hat * jnp.mean(g * hat, axis=-1, keepdims=True))


LEVEL_AT = ((1, 1), (0, 0), (0, 1), (1, 0))


def pack_kernel(tok, cot, pmap, cmap, dn, rt, lf, dr, dl, here, rows, wide, narrow):
    for i in range(72):
        rows[4 * i : 4 * i + 4] = cot[i].astype(F32)
    c = nn(cmap[...], rows[...].astype(BF16))
    wide[...] = jnp.zeros_like(wide)
    narrow[...] = jnp.zeros_like(narrow)
    for lev in range(4):
        top = tok[lev, 0:144]
        dn[lev, 0:144] = top
        for side, block in enumerate((tok[lev, 144:288], top)):
            got = nn(pmap[...], block)
            wide[side, lev * 54 : lev * 54 + 54] = got[0:54]
            narrow[side, lev * 18 : lev * 18 + 18] = got[56:74]
        here[lev] = c[lev * 96 : lev * 96 + 48].astype(BF16)
        part = c[lev * 96 + 48 : lev * 96 + 96].astype(BF16)
        dn[lev, 144:192] = part[:, 0:D]
        dn[lev, 192:240] = part[:, D : 2 * D]
    for side in range(2):
        part = c[384 + 24 * side : 408 + 24 * side]
        wide[side, 216:240] = part[:, 0:D]
        wide[side, 240:264] = part[:, D : 2 * D]
    rt[...] = wide[0].astype(BF16)
    dr[...] = wide[1].astype(BF16)
    lf[...] = narrow[0].astype(BF16)
    dl[...] = narrow[1].astype(BF16)


def label(pos, z, bottom):
    row = ((pos % 72 >= 36) & bottom).astype(jnp.int32)
    return row + (2 * (pos // 72).astype(jnp.int32) if z == 1 else 0)


def split_weights(wqkv, w3, wt3):
    eye = (lax.broadcasted_iota(jnp.int32, (D, D), 0) == lax.broadcasted_iota(jnp.int32, (D, D), 1)).astype(BF16)
    for part in range(3):
        w = wqkv[:, part * D : (part + 1) * D]
        w3[part] = w
        wt3[part] = nt(eye, w).astype(BF16)


def prepare_kernel(bottom_ref, wqkv, bias, w3, wt3, bias_t, side_t, low_cols, high_cols):
    split_weights(wqkv, w3, wt3)
    bottom = bottom_ref[0, 0] > 0
    lane = lax.broadcasted_iota(jnp.int32, (1, HQ), 1) % WT
    row = lax.broadcasted_iota(jnp.int32, (WT, 1), 0)
    narrow = lax.broadcasted_iota(jnp.int32, (1, WT), 1) % 24
    narrow = narrow // 12 * 72 + narrow % 12 * 6
    for z in range(2):
        bias_t[z] = jnp.where(label(row, z, bottom) != label(lane, z, bottom), OFF, bias[z].T)
        low_cols[...] = bias[z, :, 0:128]
        high_cols[:, 0 : WT - 128] = bias[z, :, 128:WT]
        for n in range(2):
            every = pl.ds(5 - 5 * n, WT, stride=6)
            table = jnp.concatenate([low_cols[every, :], high_cols[every, :][:, 0 : WT - 128]], axis=1).T
            side_t[n, z] = jnp.where(label(row, z, bottom) != label(narrow, z, bottom), OFF, table)


def staged(kernel, inputs, scalar_count=0):
    def run(*refs):
        scalars, refs = refs[:scalar_count], refs[scalar_count:]
        fetched, rest = refs[:inputs], refs[inputs:]
        places, sems, rest = rest[-inputs - 1 : -1], rest[-1], rest[: -inputs - 1]
        copies = [pltpu.make_async_copy(a, b, sems.at[n]) for n, (a, b) in enumerate(zip(fetched, places))]
        for copy in copies:
            copy.start()

        def arrive(first, last):
            for copy in copies[first:last]:
                copy.wait()

        kernel(arrive, *scalars, *places, *rest)

    return run


def first_kernel(
    arrive, core_ref, own, dn, rt, lf, dr, dl, m_win, gain_one,
    w3, wt3, bias_t, side_t,
    m_head, wproj, m_side, m_sidet, m_sfold, m_pick, m_there,
    m_quad, cot, m_cot, gain_two, wfc1, wfc2t, gain_merge, wmerge, m_back,
    stay, leave, merged, tok8_out, xn_out, prob_out, dout,
    tok8, xn, prob, sent, grads, halo, mixed, tok, side, resq, mlpin, act, dgel, blk, dblk, dpres, dresq, resw, cotq,
):
    arrive(0, 8)

    halo[...] = jnp.zeros_like(halo)
    rt_, lf_, dr_, dl_ = (ref[...].astype(F32) for ref in (rt, lf, dr, dl))
    for lev in range(4):
        z, li = LEVEL_AT[lev]
        halo[0:54] = rt_[lev * 54 : lev * 54 + 54]
        halo[56:74] = lf_[lev * 18 : lev * 18 + 18]
        halo[80:134] = dr_[lev * 54 : lev * 54 + 54]
        halo[136:154] = dl_[lev * 18 : lev * 18 + 18]
        src = jnp.concatenate([own[lev, 144:288], dn[lev, 0:144], halo[...].astype(BF16)], axis=0)
        got = nn(m_win[...], src)
        for win in range(6):
            tok[z * 6 + win, li * 72 : li * 72 + 72] = got[win * 72 : win * 72 + 72]

    g1 = gain_one[...]

    arrive(8, 19)

    def forward(i, carry):
        ws = [i * GROUP + n for n in range(GROUP)]
        zs = [w // 4 for w in ws]
        ts = [tok[z * 6 + w % 4 + 1] for w, z in zip(ws, zs)]
        xs = [(norm_parts(t)[0] * g1).astype(BF16) for t in ts]
        for w, t, x in zip(ws, ts, xs):
            tok8[w] = t.astype(BF16)
            xn[w] = x
        qs = [nn(x, w3[0]).astype(BF16) for x in xs]
        ks = [nn(x, w3[1]).astype(BF16) for x in xs]
        vts = [nt(wt3[2], x).astype(BF16) for x in xs]
        ss = [nt(k, jnp.concatenate([q] * HEADS, axis=0) * m_head[...]) for q, k in zip(qs, ks)]
        ps = []
        for w, z, score in zip(ws, zs, ss):
            e = jnp.exp(score * SCALE + bias_t[z])
            p = (e * (1.0 / jnp.sum(e, axis=0, keepdims=True))).astype(BF16)
            prob[w] = p
            ps.append(p)
        mxs = [by_head(vt, p).astype(BF16) for vt, p in zip(vts, ps)]
        for w, t, mx in zip(ws, ts, mxs):
            mixed[w] = mx
            att = nn(mx, wproj[...]).astype(BF16)
            resw[w] = (t + att.astype(F32)).astype(BF16).astype(F32)
        return carry

    forward(0, 0)
    early = [
        pltpu.make_async_copy(a, b, sent.at[n]) for n, (a, b) in enumerate(((tok8, tok8_out), (xn, xn_out), (prob, prob_out)))
    ]
    for copy in early:
        copy.start()

    beside = [(n, z) for n in range(2) for z in range(2)]
    ts = [tok[z * 6 + 5 * n] for n, z in beside]
    xs = [(norm_parts(t)[0] * g1).astype(BF16) for t in ts]
    qs = [nn(x, w3[0]).astype(BF16) for x in xs]
    ks = [nn(x, w3[1]).astype(BF16) for x in xs]
    vts = [nt(wt3[2], x).astype(BF16) for x in xs]
    ss = [nt(k, nn(m_pick[n], q).astype(BF16) * m_side[...]) for q, k, (n, z) in zip(qs, ks, beside)]
    ps = []
    for score, (n, z) in zip(ss, beside):
        e = jnp.exp(score * SCALE + side_t[n, z])
        ps.append((e * (1.0 / jnp.sum(e, axis=0, keepdims=True))).astype(BF16))
    fulls = [nn(vt, p).astype(BF16) * m_sidet[...] for vt, p in zip(vts, ps)]
    mxs = [nt(m_sfold[...], full).astype(BF16) for full in fulls]
    for t, mx, (n, z) in zip(ts, mxs, beside):
        att = nn(mx, wproj[...]).astype(BF16)
        there = nn(m_there[n], t.astype(BF16))
        side[n, z] = (there + att.astype(F32)).astype(BF16)

    arrive(19, 28)

    for lev in range(4):
        z, li = LEVEL_AT[lev]
        src = jnp.concatenate([resw[z * 4 + win, li * 72 : li * 72 + 72] for win in range(4)], axis=0).astype(BF16)
        src = jnp.concatenate([src, side[0, z, li * 16 : li * 16 + 16], side[1, z, li * 16 : li * 16 + 16]], axis=0)
        got = nn(m_quad[...], src).astype(BF16)
        for k in range(4):
            resq[k, lev * 80 : lev * 80 + 80] = got[k * 80 : k * 80 + 80]

    src = []
    for lev in range(4):
        src += [cot[lev], jnp.concatenate([dn[lev, 144:192], dn[lev, 192:240]], axis=1)]
    for block in (rt_, dr_):
        src.append(jnp.concatenate([block[216:240], block[240:264]], axis=1))
    src = jnp.concatenate(src[:8] + [jnp.concatenate(src[8:], axis=0).astype(BF16)], axis=0)
    cotq[...] = nn(m_cot[...], src).astype(BF16)

    g2 = gain_two[...]
    inner = np.float32(np.sqrt(2 / np.pi))

    def feed(k):
        res = resq[k].astype(F32)
        hat, _ = norm_parts(res)
        mi = (hat * g2).astype(BF16)
        mlpin[k] = mi
        pre = nn(mi, wfc1[...])
        sq = pre * pre
        t = jnp.tanh(pre * (inner + (inner * 0.044715) * sq))
        half = 0.5 + 0.5 * t
        full = pre * half
        a = full.astype(BF16)
        act[k] = a
        dgel[k] = half + full * (1.0 - half) * (2 * inner + (6 * inner * 0.044715) * sq)
        blk[k] = (res + nt(a, wfc2t[...])).astype(BF16)

    for k in range(4):
        feed(k)

    total = 0.0
    for k in range(4):
        total = total + jnp.sum(blk[k].astype(F32), axis=-1, keepdims=True)
    mean = total * (1.0 / 768)
    total = 0.0
    for k in range(4):
        center = blk[k].astype(F32) - mean
        total = total + jnp.sum(center * center, axis=-1, keepdims=True)
    rstd = lax.rsqrt(total * (1.0 / 768) + EPS)
    cq = cotq[...]
    pair = lax.broadcasted_iota(jnp.int32, (320, MG), 0) % 80 % 13
    cq_own = jnp.where(pair < 12, cq.astype(F32), 0.0).astype(BF16)
    out = 0.0
    sum_a = 0.0
    sum_b = 0.0
    hats, gs = [], []
    for k in range(4):
        gm = gain_merge[:, k * D : k * D + D]
        hat = (blk[k].astype(F32) - mean) * rstd
        mn = (hat * gm).astype(BF16)
        wm = wmerge[k * D : k * D + D]
        out = out + nn(mn, wm)
        gmerge = tn(mn, cq_own).astype(BF16)
        for t in range(3):
            at = t * 768 + k * D
            grads[1, at : at + D] = gmerge[:, t * 128 : t * 128 + 128]
        g = nt(cq, wm) * gm
        hats.append(hat)
        gs.append(g)
        sum_a = sum_a + jnp.sum(g, axis=-1, keepdims=True)
        sum_b = sum_b + jnp.sum(g * hat, axis=-1, keepdims=True)
    merged[...] = out.astype(BF16)
    sum_a = sum_a * (1.0 / 768)
    sum_b = sum_b * (1.0 / 768)
    pair = lax.broadcasted_iota(jnp.int32, (320, D), 0) % 80 % 13
    for k in range(4):
        d = rstd * (gs[k] - sum_a - hats[k] * sum_b)
        d = jnp.where(pair == (0 if k % 2 == 0 else 12), 0.0, d)
        db = d.astype(BF16)
        dpre = (nn(db, wfc2t[...]) * dgel[k]).astype(BF16)
        dblk[k] = db
        dpres[k] = dpre
        dmlp = nt(dpre, wfc1[...])
        hat2, rstd2 = norm_parts(resq[k].astype(F32))
        dresq[k] = (db.astype(F32) + norm_back(hat2, rstd2, g2, dmlp)).astype(BF16)
    fc1 = tn(mlpin[...].reshape(1280, D), dpres[...].reshape(1280, FF))
    fc2 = tn(dblk[...].reshape(1280, D), act[...].reshape(1280, FF))
    for base, value in ((0, fc1.astype(BF16)), (1152, fc2.astype(BF16))):
        for t in range(6):
            grads[0, base + t * D : base + t * D + D] = value[:, t * 128 : t * 128 + 128]

    for lev in range(4):
        z, li = LEVEL_AT[lev]
        src = jnp.concatenate([dresq[k, lev * 80 : lev * 80 + 80] for k in range(4)], axis=0)
        got = nn(m_back[...], src)
        for win in range(4):
            resw[z * 4 + win, li * 72 : li * 72 + 72] = got[win * 72 : win * 72 + 72]
    dout[...] = resw[...].astype(BF16)
    grads[:, 2304:HALF] = jnp.zeros((2, HALF - 2304, 128), BF16)
    gproj = tn(mixed[...].reshape(8 * WT, D), dout[...].reshape(8 * WT, D)).astype(BF16)
    grads[0, 2304 : 2304 + D] = gproj[:, 0:128]
    grads[1, 2304 : 2304 + D, 0:64] = gproj[:, 128:192]
    core = core_ref[0, 0]
    stay[...] = grads[core]
    leave[...] = grads[1 - core]
    for copy in early:
        copy.wait()


def second_kernel(
    arrive, w3, wt3, wproj, xn, datt, m_head, prob,
    grads, dqkv,
    gb,
):
    gb[...] = jnp.zeros_like(gb)
    arrive(0, 6)

    def backward(i, carry):
        ws = [i * GROUP + n for n in range(GROUP)]
        xs = [xn[w] for w in ws]
        ups = [datt[w] for w in ws]
        qs = [nn(x, w3[0]).astype(BF16) for x in xs]
        vs = [nn(x, w3[2]).astype(BF16) for x in xs]
        kts = [nt(wt3[1], x).astype(BF16) for x in xs]
        dms = [nt(up, wproj[...]).astype(BF16) for up in ups]
        dmbds = [jnp.concatenate([dm] * HEADS, axis=0) * m_head[...] for dm in dms]
        dps = [nt(v, dmbd) for v, dmbd in zip(vs, dmbds)]
        arrive(6, 7)
        dsbs = []
        for w, dp in zip(ws, dps):
            p = prob[w].astype(F32)
            ds = p * (dp - jnp.sum(dp * p, axis=0, keepdims=True))
            gb[w // 4] += ds
            dsbs.append((ds * SCALE).astype(BF16))
        for w, dmbd in zip(ws, dmbds):
            dqkv[2, w] = nn(prob[w], dmbd).astype(BF16)
        qbds = [jnp.concatenate([q] * HEADS, axis=0) * m_head[...] for q in qs]
        for w, dsb, qbd in zip(ws, dsbs, qbds):
            dqkv[1, w] = nn(dsb, qbd).astype(BF16)
        for w, kt, dsb in zip(ws, kts, dsbs):
            dqkv[0, w] = by_head(kt, dsb).astype(BF16)
        return carry

    backward(0, 0)

    xs = xn[...].reshape(8 * WT, D)
    parts = [tn(xs, dqkv[part].reshape(8 * WT, D)) for part in range(3)]
    value = jnp.concatenate(parts, axis=1).astype(BF16)
    def put(start, block):
        for n in range(block.shape[0] // SECOND):
            grads[start // SECOND + n, 0:SECOND] = block[n * SECOND : n * SECOND + SECOND]

    for t in range(4):
        put(t * D, value[:, t * 128 : t * 128 + 128])
    put(768, jnp.concatenate([value[:, 512:576], jnp.zeros((D, 64), BF16)], axis=1))
    for z in range(2):
        total = gb[z].astype(BF16)
        for t in range(7):
            tile = total[:, t * 128 : min(t * 128 + 128, HQ)]
            if t == 6:
                tile = jnp.concatenate([tile, jnp.zeros((WT, 896 - HQ), BF16)], axis=1)
            put(BIAS_AT + (z * 7 + t) * WT, tile)
    end = BIAS_AT + 14 * WT
    put(end, jnp.zeros((PEERS * SECOND - end, 128), BF16))


def third_kernel(
    tok8, datt, dqkv, merged, gain_one, wqkv, m_out, m_merged,
    keep_t, keep_m, to_rt, to_dn, to_dr,
    gt,
):
    g1 = gain_one[...]
    ws = [wqkv[:, part * D : (part + 1) * D] for part in range(3)]
    for w in range(8):
        dnorm = (nt(dqkv[0, w], ws[0]) + nt(dqkv[1, w], ws[1]) + nt(dqkv[2, w], ws[2])).astype(BF16).astype(F32)
        hat, rstd = norm_parts(tok8[w].astype(F32))
        gt[w] = (datt[w].astype(F32) + norm_back(hat, rstd, g1, dnorm)).astype(BF16).astype(F32)

    for lev in range(4):
        z, li = LEVEL_AT[lev]
        src = jnp.concatenate([gt[z * 4 + win, li * 72 : li * 72 + 72] for win in range(4)], axis=0).astype(BF16)
        got = nn(m_out[...], src).astype(BF16)
        keep_t[lev] = got[0:144]
        to_dn[lev, 0:144] = got[144:288]
        to_rt[lev, 0:32] = got[288:320]
        to_dr[lev, 0:32] = got[320:352]
        got = nn(m_merged[...], merged[lev * 80 : lev * 80 + 80]).astype(BF16)
        keep_m[lev] = got[0:48]
        for half in range(2):
            part = got[:, half * D : half * D + D]
            to_dn[lev, 144 + 48 * half : 192 + 48 * half] = part[48:96]
            to_rt[lev, 32 + 16 * half : 48 + 16 * half] = part[96:112]
            to_dr[lev, 32 + 16 * half : 48 + 16 * half] = part[112:128]


def place_kernel(keep_t, keep_m, rt, dn, dr, m_place, m_pm, grad_tokens, merged):
    def halves(ref, lev, start, count):
        return jnp.concatenate([ref[lev, start : start + count], ref[lev, start + count : start + 2 * count]], axis=1)

    for lev in range(4):
        low = keep_t[lev].astype(F32) + nn(m_place[...], rt[lev, 0:32])
        top = dn[lev, 0:144].astype(F32) + nn(m_place[...], dr[lev, 0:32])
        grad_tokens[lev, 0:144] = top.astype(BF16)
        grad_tokens[lev, 144:288] = low.astype(BF16)
    src = [keep_m[lev] for lev in range(4)]
    src += [halves(dn, lev, 144, 48) for lev in range(4)]
    src += [halves(rt, lev, 32, 16) for lev in range(4)]
    src += [halves(dr, lev, 32, 16) for lev in range(4)]
    got = nn(m_pm[...], jnp.concatenate(src, axis=0)).astype(BF16)
    for i in range(72):
        merged[i] = got[4 * i : 4 * i + 4]


def add_kernel(is_weight, got, out, *, bands):
    count = got.shape[0]
    mine = got[0, SECOND:ROWS].astype(F32)
    for n in range(1, count):
        mine = mine + got[n, SECOND:ROWS].astype(F32)
    mine = mine.astype(BF16)
    total = 0.0
    parts = []
    for b in range(bands):
        part = got[b, 0:SECOND].astype(F32)
        for n in range(b + bands, count, bands):
            part = part + got[n, 0:SECOND].astype(F32)
        parts.append(part)
        total = total + part
    flag = is_weight[0, 0] > 0
    for b in range(bands):
        part = jnp.where(flag, total, parts[b]).astype(BF16)
        for n in range(b, count, bands):
            out[n, SECOND:ROWS] = mine
            out[n, 0:SECOND] = part


def pieces(start, count, size):
    while count:
        chunk, off = start // size, start % size
        take = min(count, size - off)
        yield chunk, off, take
        start, count = start + take, count - take


def bias_kernel(buf, gbias, *, scale):
    def rows(start, count):
        got = [buf[c, off : off + n].astype(F32) for c, off, n in pieces(start, count, SECOND)]
        return jnp.concatenate(got, axis=0)

    for z in range(2):
        for t in range(7):
            part = rows(BIAS_AT + (z * 7 + t) * WT, WT).T * scale
            end = min(t * 128 + 128, HQ)
            gbias[z, t * 128 : end] = part[0 : end - t * 128]


def final_kernel(core_ref, buf, oth, gqkv, gproj, gfc1, gfc2t, gmerge, *, scale):
    here = core_ref[0, 0]

    def first(half, start, count):
        got = []
        for c, off, n in pieces(start, count, FIRST):
            at = SECOND + off
            got.append(jnp.where(here == half, buf[c, at : at + n], oth[c, at : at + n]).astype(F32))
        return jnp.concatenate(got, axis=0) * scale

    def second(start, count):
        got = []
        for c, off, n in pieces(start, count, SECOND):
            got.append(buf[c, off : off + n].astype(F32) + oth[c, off : off + n].astype(F32))
        return jnp.concatenate(got, axis=0) * scale

    for t in range(6):
        gfc1[:, t * 128 : t * 128 + 128] = first(0, t * D, D)
        gfc2t[:, t * 128 : t * 128 + 128] = first(0, 1152 + t * D, D)
    for t in range(3):
        gmerge[:, t * 128 : t * 128 + 128] = first(1, t * 768, 768)
    gproj[:, 0:128] = first(0, 2304, D)
    gproj[:, 128:192] = first(1, 2304, D)[:, 0:64]
    for t in range(5):
        end = min(t * 128 + 128, 576)
        gqkv[:, t * 128 : end] = second(t * D, D)[:, 0 : end - t * 128]


def call(kernel, outs, scratch=(), flops=10**7, size=10**6, limit=16, **more):
    return pl.pallas_call(
        kernel,
        out_shape=outs,
        **more,
        scratch_shapes=list(scratch),
        compiler_params=pltpu.CompilerParams(vmem_limit_bytes=limit * 2**20),
        cost_estimate=pl.CostEstimate(flops=flops, bytes_accessed=size, transcendentals=0),
    )


def shape(*dims, kind=BF16):
    return jax.ShapeDtypeStruct(dims, kind)


def first_call():
    held = pl.BlockSpec(memory_space=pltpu.HBM)
    operands = [
        shape(4, 288, D),
        shape(4, 240, D),
        shape(272, D),
        shape(80, D),
        shape(272, D),
        shape(80, D),
        shape(432, 448),
        shape(1, D, kind=F32),
        shape(3, D, D),
        shape(3, D, D),
        shape(2, WT, HQ, kind=F32),
        shape(2, 2, WT, WT, kind=F32),
        shape(HQ, D),
        shape(D, D),
        shape(WT, D),
        shape(D, WT),
        shape(32, WT),
        shape(2, WT, WT),
        shape(2, 32, WT),
        shape(320, 320),
        shape(4, 48, MG),
        shape(320, 432),
        shape(1, D, kind=F32),
        shape(D, FF),
        shape(D, FF),
        shape(1, FF, kind=F32),
        shape(FF, MG),
        shape(288, 320),
    ]
    count = len(operands)
    return call(
        staged(first_kernel, count, 1),
        (
            shape(HALF, 128),
            shape(HALF, 128),
            shape(320, MG),
            shape(8, WT, D),
            shape(8, WT, D),
            shape(8, WT, HQ),
            shape(8, WT, D),
        ),
        [
            pltpu.VMEM((8, WT, D), BF16),
            pltpu.VMEM((8, WT, D), BF16),
            pltpu.VMEM((8, WT, HQ), BF16),
            pltpu.SemaphoreType.DMA((3,)),
            pltpu.VMEM((2, HALF, 128), BF16),
            pltpu.VMEM((160, D), F32),
            pltpu.VMEM((8, WT, D), BF16),
            pltpu.VMEM((12, WT, D), F32),
            pltpu.VMEM((2, 2, 32, D), BF16),
            pltpu.VMEM((4, 320, D), BF16),
            pltpu.VMEM((4, 320, D), BF16),
            pltpu.VMEM((4, 320, FF), BF16),
            pltpu.VMEM((4, 320, FF), F32),
            pltpu.VMEM((4, 320, D), BF16),
            pltpu.VMEM((4, 320, D), BF16),
            pltpu.VMEM((4, 320, FF), BF16),
            pltpu.VMEM((4, 320, D), BF16),
            pltpu.VMEM((8, WT, D), F32),
            pltpu.VMEM((320, MG), BF16),
        ]
        + [pltpu.VMEM(op.shape, op.dtype) for op in operands]
        + [pltpu.SemaphoreType.DMA((count,))],
        flops=2 * 10**10,
        size=10**7,
        limit=58,
        in_specs=[SCALAR] + [held] * count,
        out_specs=(WHOLE, WHOLE, WHOLE, held, held, held, WHOLE),
    )


def second_call():
    operands = [
        shape(3, D, D),
        shape(3, D, D),
        shape(D, D),
        shape(8, WT, D),
        shape(8, WT, D),
        shape(HQ, D),
        shape(8, WT, HQ),
    ]
    count = len(operands)
    return call(
        staged(second_kernel, count),
        (shape(PEERS, ROWS, 128), shape(3, 8, WT, D)),
        [
            pltpu.VMEM((2, WT, HQ), F32),
        ]
        + [pltpu.VMEM(op.shape, op.dtype) for op in operands]
        + [pltpu.SemaphoreType.DMA((count,))],
        flops=10**10,
        size=10**7,
        limit=58,
        in_specs=[pl.BlockSpec(memory_space=pltpu.HBM)] * count,
    )


def third_call():
    return call(
        third_kernel,
        (shape(4, 144, D), shape(4, 48, MG), shape(4, 64, D), shape(4, 240, D), shape(4, 64, D)),
        [pltpu.VMEM((8, WT, D), F32)],
        flops=10**10,
        size=10**7,
        limit=58,
    )


def body(tokens, gain_one, w_qkv, w_proj, bias_table, gain_two, w_fc1, w_fc2, gain_merge, w_merge, cotangent):
    lat_count = lax.axis_size(LAT)
    lon_count = lax.axis_size("lon")
    count = lat_count * lon_count
    peers = ("lon", "chip")
    bottom = (lax.axis_index(LAT) == lat_count - 1).astype(jnp.int32).reshape(1, 1)
    core = lax.axis_index("core").reshape(1, 1)
    flat = tokens.reshape(4, 288, D)

    def move(block, lon_step, lat_step):
        route = []
        for a in range(lon_count):
            for b in range(lat_count):
                to = (a + lon_step) % lon_count * lat_count + (b + lat_step) % lat_count
                route.append((a * lat_count + b, to))
        return lax.ppermute(block, ("lon",) + LAT, route)

    dn, rt, lf, dr, dl, cot = call(
        pack_kernel,
        (
            shape(4, 240, D),
            shape(272, D),
            shape(80, D),
            shape(272, D),
            shape(80, D),
            shape(4, 48, MG),
        ),
        [pltpu.VMEM((288, MG), F32), pltpu.VMEM((2, 272, D), F32), pltpu.VMEM((2, 80, D), F32)],
        limit=58,
    )(flat, cotangent.transpose(1, 2, 0, 3).reshape(72, 4, MG), pack_map(), pack_cot_map())
    dn = move(dn, 0, -1)
    rt = move(rt, -1, 0)
    lf = move(lf, 1, 0)
    dr = move(dr, -1, -1)
    dl = move(dl, 1, -1)

    head, sidem = head_mask(), side_mask()
    g1 = gain_one.reshape(1, D)
    w3, wt3, bias_t, side_t = call(
        prepare_kernel,
        (shape(3, D, D), shape(3, D, D), shape(2, WT, HQ, kind=F32), shape(2, 2, WT, WT, kind=F32)),
        [pltpu.VMEM((HQ, 128), F32), pltpu.VMEM((HQ, 128), F32)],
        limit=58,
        in_specs=[SCALAR, WHOLE, WHOLE],
    )(bottom, w_qkv, bias_table.reshape(2, HQ, WT))
    first, leave, merged, tok8, xn, prob, datt = first_call()(
        core, flat, dn, rt, lf, dr, dl, window_map(), g1, w3, wt3, bias_t, side_t,
        head, w_proj, sidem, sidem.T, side_fold(),
        jnp.stack([side_pick(5, False), side_pick(0, False)]), jnp.stack([side_pick(5, True), side_pick(0, True)]),
        quad_map(), cot, cot_map(), gain_two.reshape(1, D), w_fc1, w_fc2.T, gain_merge.reshape(1, FF), w_merge, back_map(),
    )
    arrived = lax.ppermute(leave, "core", [(0, 1), (1, 0)])
    grads, dqkv = second_call()(w3, wt3, w_proj, xn, datt, head, prob)
    arrived, grads = lax.optimization_barrier((arrived, grads))
    first = (first.astype(F32) + arrived.astype(F32)).astype(BF16).reshape(PEERS, FIRST, 128)
    grads = lax.dynamic_update_slice(grads, first, (0, SECOND, 0))
    grads = lax.all_to_all(grads, peers, 0, 0)
    keep_t, keep_m, rt, dn, dr = third_call()(tok8, datt, dqkv, merged, g1, w_qkv, out_map(), merged_map())
    rt = move(rt, 1, 0)
    dn = move(dn, 0, 1)
    dr = move(dr, 1, 1)
    grads, keep_t = lax.optimization_barrier((grads, keep_t))
    place = lax.axis_index(peers)
    is_weight = (place < BIAS_AT // SECOND).astype(jnp.int32).reshape(1, 1)
    grads = call(
        functools.partial(add_kernel, bands=lax.axis_size("chip")), shape(PEERS, ROWS, 128), in_specs=[SCALAR, WHOLE]
    )(is_weight, grads)
    grads = lax.all_to_all(grads, peers, 0, 0)
    grads, rt, dn, dr = lax.optimization_barrier((grads, rt, dn, dr))
    grad_tokens, merged = call(place_kernel, (shape(4, 288, D), shape(72, 4, MG)))(
        keep_t, keep_m, rt, dn, dr, place_map(), place_merged_map()
    )
    other = lax.ppermute(grads, "core", [(0, 1), (1, 0)])
    gbias = call(
        functools.partial(bias_kernel, scale=WT * (4 * lon_count) ** (-0.5)), shape(2, HQ, WT, kind=F32)
    )(grads)
    gqkv, gproj, gfc1, gfc2t, gmerge = call(
        functools.partial(final_kernel, scale=(1152 * count) ** (-0.5)),
        (
            shape(D, 3 * D, kind=F32),
            shape(D, D, kind=F32),
            shape(D, FF, kind=F32),
            shape(D, FF, kind=F32),
            shape(FF, MG, kind=F32),
        ),
        in_specs=[SCALAR, WHOLE, WHOLE],
    )(core, grads, other)
    return (
        merged.reshape(6, 12, 4, MG).transpose(2, 0, 1, 3),
        grad_tokens.reshape(4, 12, 24, D),
        gqkv,
        gproj,
        gfc1,
        gfc2t.T,
        gmerge,
        gbias.reshape(1, 2, HEADS, WT, WT),
    )


def solution(mesh):
    lons, lats = mesh.devices.shape
    mesh = jax.sharding.Mesh(mesh.devices.reshape(lons, lats // 2, 2), ("lon",) + LAT)
    placed = (
        P(None, LAT, "lon", None),
        P(),
        P(),
        P(),
        P(LAT, None, None, None, None),
        P(),
        P(),
        P(),
        P(),
        P(),
        P(None, LAT, "lon", None),
    )
    return jax.shard_map(
        body,
        mesh=mesh,
        in_specs=placed,
        out_specs=(
            P(None, LAT, "lon", None),
            P(None, LAT, "lon", None),
            P(),
            P(),
            P(),
            P(),
            P(),
            P(LAT, None, None, None, None),
        ),
        check_vma=False,
    )
```
